128 devices in a mesh: tm: 16 (over z, y), lm: 8 (over x, core).
Axes of the slice: x: 4, y: 4, z: 4, core: 2. Of those that a mesh axis runs over, the one named last changes fastest.
Arguments:
- knot_right_side: float32 [6, 256, 128], P(None, 'tm')
- land_rhs: float32 [3, 524288], P(None, ('tm', 'lm'))
- jac_knot: bfloat16 [12288, 32, 384], P(('tm', 'lm')), may hold values from -0.21875 to 0.21875
- jac_land: bfloat16 [12288, 32, 192], P(('tm', 'lm')), may hold values from -0.5 to 0.5
- obs_knot: int32 [12288], P(('tm', 'lm')), may hold values from 0 to 31
- obs_slot: int32 [12288], P(('tm', 'lm')), may hold values from 0 to 255
- obs_count: int32 [12288], P(('tm', 'lm')), may hold values from 8 to 32
- send_list: int32 [128, 128, 2], P(('tm', 'lm')), may hold values from 0 to 63
- couple: float32 [6, 6, 256, 128], P(None, None, 'tm')
- knot_dinv: float32 [6, 6, 256, 128], P(None, None, 'tm')
- cuts: int32 [256, 128], P('tm'), may hold values 0 or 1
- land_pinv: float32 [3, 3, 524288], P(None, None, ('tm', 'lm'))
- knot_damp: float32 [6, 256, 128], P(None, 'tm'), may hold values from 0.3 to 3
- land_damp: float32 [3, 524288], P(None, ('tm', 'lm')), may hold values from 0.3 to 3
Outputs:
- knot_step: float32 [6, 256, 128], P(None, 'tm')
- land_step: float32 [3, 524288], P(None, ('tm', 'lm'))
- knot_resid: float32 [6, 256, 128], P(None, 'tm')
- land_resid: float32 [3, 524288], P(None, ('tm', 'lm'))
The draws below stay inside these ranges and needn't reach their ends.
Inputs may be any that keep to these rules, and one draw needn't show every extreme that they name: send_list[s, d, c] is the local landmark block of device s that device s places into its slot c for device d; blocks may repeat. Observation block o sees the landmark block that device obs_slot[o] // 2 places into slot obs_slot[o] % 2 for device o // 96. obs_knot[o] = j names the knot block of vehicles 4 * j to 4 * j + 3 on the time index o // 768.
All inputs are finite; a program needn't handle non-finite values. No bound on the sum of `cuts` on one device may be relied on, other than what follows from the above.
Results may differ from the reference program's by a relative error of at most 0.00115.
Values may be sent and summed in bfloat16 or wider, within the bound.
A program may use at most 192 MiB of HBM per device.

```python
import math
import jax
import jax.numpy as jnp
from jax import lax

VEHICLE_TOTAL = 128
VB = 4
K_DEV = 16
LB = 64
LB_DEV = 64
R = 32
B_DEV = 96
ITERS = 3
SPLINE_POINTS = 256
KB_DEV = 32
KW = 384
LW = 192
SENDERS = 128
NLB = 8192
NL = 524288
NOB = 12288
CAP = 2
SLOTS = 256
N_TM = 16
N_LM = 8


def draw_couple(key, part):
    seeded_generators = jax.random.split(jax.random.fold_in(key, 11), 5)
    lengths = jnp.exp(jax.random.uniform(seeded_generators[0], (6, 1, VEHICLE_TOTAL), minval=math.log(20.0), maxval=math.log(4.0 * SPLINE_POINTS)))
    jitter = jax.random.uniform(seeded_generators[1], (6, SPLINE_POINTS, VEHICLE_TOTAL), minval=0.5, maxval=2.0)
    frequency_levels = jnp.exp(-jitter / lengths)
    clustered_batches = jax.random.uniform(seeded_generators[2], (1, SPLINE_POINTS, VEHICLE_TOTAL)) < 3.0 / SPLINE_POINTS
    magnitude_multiplier = jax.random.uniform(seeded_generators[3], (1, SPLINE_POINTS, VEHICLE_TOTAL), minval=0.5, maxval=0.8)
    frequency_levels = jnp.where(clustered_batches, frequency_levels * magnitude_multiplier, frequency_levels)
    skew = jax.random.normal(seeded_generators[4], (SPLINE_POINTS, VEHICLE_TOTAL, 6, 6)) * 0.35
    skew = skew - jnp.swapaxes(skew, -1, -2)
    unit = jnp.broadcast_to(jnp.eye(6, dtype=jnp.float32), (SPLINE_POINTS, VEHICLE_TOTAL, 6, 6))
    rotation = jnp.linalg.solve(unit - skew, unit + skew)
    rotation = jnp.transpose(rotation, (2, 3, 0, 1))
    return (frequency_levels[:, None, :, :] * rotation).astype(jnp.float32)


def draw_knot_dinv(key, part):
    seeded_generators = jax.random.split(jax.random.fold_in(key, 23), 2)
    base = jax.random.normal(seeded_generators[0], (SPLINE_POINTS, VEHICLE_TOTAL, 6, 6))
    inner = jnp.einsum('kvab,kvcb->kvac', base, base) / 6.0 + 0.6 * jnp.eye(6, dtype=jnp.float32)
    scale = 4.0 / math.sqrt(SPLINE_POINTS) * jnp.exp(jax.random.uniform(seeded_generators[1], (SPLINE_POINTS, VEHICLE_TOTAL), minval=0.0, maxval=math.log(4.0)))
    return jnp.transpose(inner * scale[:, :, None, None], (2, 3, 0, 1)).astype(jnp.float32)


def draw_land_pinv(key, part):
    seeded_generators = jax.random.split(jax.random.fold_in(key, 37), 2)
    base = jax.random.normal(seeded_generators[0], (NL, 3, 3))
    inner = jnp.einsum('nab,ncb->nac', base, base) / 3.0 + 0.5 * jnp.eye(3, dtype=jnp.float32)
    scale = jnp.exp(jax.random.uniform(seeded_generators[1], (NL,), minval=math.log(0.3), maxval=math.log(1.5)))
    return jnp.transpose(inner * scale[:, None, None], (1, 2, 0)).astype(jnp.float32)


def draw_knot_right_side(key, part):
    seeded_generators = jax.random.split(jax.random.fold_in(key, 41), 3)
    position = jnp.arange(SPLINE_POINTS, dtype=jnp.float32) / (SPLINE_POINTS - 1)
    ramp = (1.0 + 2.0 * position)[None, :, None]
    vehicle_scale = jnp.exp(jax.random.uniform(seeded_generators[0], (1, 1, VEHICLE_TOTAL), minval=math.log(0.3), maxval=math.log(3.0)))
    channel_scale = jnp.exp(jax.random.uniform(seeded_generators[1], (6, 1, 1), minval=0.0, maxval=math.log(3.0)))
    values = jax.random.normal(seeded_generators[2], (6, SPLINE_POINTS, VEHICLE_TOTAL)) * ramp
    return (values * vehicle_scale * channel_scale).astype(jnp.float32)


def draw_land_rhs(key, part):
    seeded_generators = jax.random.split(jax.random.fold_in(key, 53), 3)
    position = jnp.arange(NL, dtype=jnp.float32) / (NL - 1)
    ramp = (1.0 + 2.0 * position)[None, :]
    landmark_spread = jnp.exp(jax.random.uniform(seeded_generators[0], (1, NL), minval=math.log(0.3), maxval=math.log(3.0)))
    channel_scale = jnp.exp(jax.random.uniform(seeded_generators[1], (3, 1), minval=0.0, maxval=math.log(3.0)))
    values = jax.random.normal(seeded_generators[2], (3, NL)) * ramp
    return (values * landmark_spread * channel_scale).astype(jnp.float32)


def place_ends(entries, key, least, high):
    longest = entries.shape.index(max(entries.shape))
    spots = []
    for shift in (0, 1):
        where = [jax.random.randint(jax.random.fold_in(key, axis), (), 0, length) for axis, length in enumerate(entries.shape)]
        where[longest] = (where[longest] + shift) % entries.shape[longest]
        spots.append(tuple(where))
    return entries.at[spots[0]].set(least).at[spots[1]].set(high)


def levels(rng, shape, cuts, least, high):
    gain = 1.0
    for dim, shards_of in cuts:
        heights = jax.random.uniform(jax.random.fold_in(jax.random.fold_in(rng, 6), dim), (shards_of,), jnp.float32, least / len(cuts), high / len(cuts))
        gain = gain * jnp.repeat(jnp.exp(heights), shape[dim] // shards_of).reshape((-1,) + (1,) * (len(shape) - 1 - dim))
    return gain


def centred(own_key, dims, width, limit, pieces=(), kind=jnp.bfloat16):
    values = jax.random.normal(own_key, dims, jnp.float32) * width
    if len(pieces) > 0:
        values = levels(own_key, dims, pieces, -0.22, 0.18) * values
    return jnp.clip(values, min=-limit, max=limit).astype(kind)


def setup_inputs(seed: int = 0) -> dict:
    streams_of = jax.random.split(jax.random.key(seed), 15)
    knot_right_side = draw_knot_right_side(jax.random.fold_in(streams_of[14], 71), 0)
    land_rhs = draw_land_rhs(jax.random.fold_in(streams_of[14], 71), 0)
    jac_knot = centred(streams_of[2], (NOB, R, KW), (R * 24) ** -0.5, 0.21875, ((0, 128),))
    jac_land = centred(streams_of[3], (NOB, R, LW), (R * 4) ** -0.5, 0.5, ((0, 128),))
    obs_knot = place_ends(jax.random.randint(streams_of[4], (NOB,), 0, KB_DEV), jax.random.fold_in(streams_of[4], 1), 0, KB_DEV - 1).astype(jnp.int32)
    obs_slot = place_ends(jax.random.randint(streams_of[5], (NOB,), 0, SLOTS), jax.random.fold_in(streams_of[5], 1), 0, SLOTS - 1).astype(jnp.int32)
    obs_count = place_ends(jax.random.randint(streams_of[6], (NOB,), R // 4, R + 1), jax.random.fold_in(streams_of[6], 1), R // 4, R).astype(jnp.int32)
    send_list = place_ends(jax.random.randint(streams_of[7], (SENDERS, SENDERS, CAP), 0, LB_DEV), jax.random.fold_in(streams_of[7], 1), 0, LB_DEV - 1).astype(jnp.int32)
    couple = draw_couple(jax.random.fold_in(streams_of[14], 71), 0)
    knot_dinv = draw_knot_dinv(jax.random.fold_in(streams_of[14], 71), 0)
    cuts = place_ends((jax.random.randint(streams_of[10], (SPLINE_POINTS, VEHICLE_TOTAL), 0, 4 * SPLINE_POINTS) < 1).astype(jnp.int32), jax.random.fold_in(streams_of[10], 1), 0, 1)
    land_pinv = draw_land_pinv(jax.random.fold_in(streams_of[14], 71), 0)
    knot_damp = jnp.clip(jnp.exp(math.log(3.0) - 2.3025851 * jax.random.uniform(streams_of[12], (6, SPLINE_POINTS, VEHICLE_TOTAL), jnp.float32) ** levels(streams_of[12], (6, SPLINE_POINTS, VEHICLE_TOTAL), ((1, 16),), -0.2, 0.2)), 0.3, 3.0)
    land_damp = jnp.clip(jnp.exp(math.log(3.0) - 2.3025851 * jax.random.uniform(streams_of[13], (3, NL), jnp.float32) ** levels(streams_of[13], (3, NL), ((1, 128),), -0.2, 0.2)), 0.3, 3.0)
    return {"knot_right_side": knot_right_side, "land_rhs": land_rhs, "jac_knot": jac_knot, "jac_land": jac_land, "obs_knot": obs_knot, "obs_slot": obs_slot, "obs_count": obs_count, "send_list": send_list, "couple": couple, "knot_dinv": knot_dinv, "cuts": cuts, "land_pinv": land_pinv, "knot_damp": knot_damp, "land_damp": land_damp}


highest = lax.Precision.HIGHEST

def knot_blocks(field):
    shaped = field.reshape(6, N_TM, K_DEV, KB_DEV, VB)
    return jnp.transpose(shaped, (1, 3, 0, 2, 4)).reshape(N_TM * KB_DEV, KW)

def knot_field(blocks):
    shaped = blocks.reshape(N_TM, KB_DEV, 6, K_DEV, VB)
    return jnp.transpose(shaped, (2, 0, 3, 1, 4)).reshape(6, SPLINE_POINTS, VEHICLE_TOTAL)

def land_blocks(field):
    return jnp.transpose(field.reshape(3, NLB, LB), (1, 0, 2)).reshape(NLB, LW)

def land_field(blocks):
    return jnp.transpose(blocks.reshape(NLB, 3, LB), (1, 0, 2)).reshape(3, NL)

def hessian_product(knot_dir, land_dir, jac_knot, jac_land, obs_knot, obs_slot, obs_count, send_list, knot_damp, land_damp):
    knot_bf = knot_blocks(knot_dir.astype(jnp.bfloat16))
    land_bf = land_blocks(land_dir.astype(jnp.bfloat16))
    row_index = jnp.arange(R, dtype=jnp.int32)

    def per_unit_term(carry, device):
        knot_acc, land_acc = carry
        first = (device * B_DEV).astype(jnp.int32)
        jac_k = lax.dynamic_slice_in_dim(jac_knot, first, B_DEV, 0).astype(jnp.float32)
        jac_l = lax.dynamic_slice_in_dim(jac_land, first, B_DEV, 0).astype(jnp.float32)
        knots_here = lax.dynamic_slice_in_dim(obs_knot, first, B_DEV, 0)
        slots_here = lax.dynamic_slice_in_dim(obs_slot, first, B_DEV, 0)
        counts_here = lax.dynamic_slice_in_dim(obs_count, first, B_DEV, 0)
        knot_index = (device // N_LM * KB_DEV + knots_here).astype(jnp.int32)
        owner = slots_here // CAP
        column = slots_here % CAP
        land_index = (owner * LB_DEV + send_list[owner, device, column]).astype(jnp.int32)
        knot_in = knot_bf[knot_index].astype(jnp.float32)
        land_in = land_bf[land_index].astype(jnp.float32)
        resid = jnp.einsum('orc,oc->or', jac_k, knot_in, precision=highest) + jnp.einsum('orc,oc->or', jac_l, land_in, precision=highest)
        mask = (row_index[None, :] < counts_here[:, None]).astype(jnp.float32)
        resid_bf = (resid * mask).astype(jnp.bfloat16).astype(jnp.float32)
        knot_terms = jnp.einsum('orc,or->oc', jac_k, resid_bf, precision=highest)
        land_terms = jnp.einsum('orc,or->oc', jac_l, resid_bf, precision=highest)
        return ((knot_acc.at[knot_index].add(knot_terms), land_acc.at[land_index].add(land_terms)), None)
    start = (jnp.zeros((N_TM * KB_DEV, KW), jnp.float32), jnp.zeros((NLB, LW), jnp.float32))
    (knot_acc, land_acc), _ = lax.scan(per_unit_term, start, jnp.arange(N_TM * N_LM, dtype=jnp.int32))
    return (knot_field(knot_acc) + knot_damp * knot_dir, land_field(land_acc) + land_damp * land_dir)

def precondition(knot_res, land_res, couple, knot_dinv, cuts, land_pinv):
    live = couple * (1 - cuts).astype(jnp.float32)[None, None]
    chain = jnp.moveaxis(live, 2, 0)
    dinv_chain = jnp.moveaxis(knot_dinv, 2, 0)

    def advance(carry, item):
        value = item[1] + carry
        return (-jnp.einsum('abv,bv->av', item[0], value, precision=highest), value)
    _, wvalues = lax.scan(advance, jnp.zeros((6, VEHICLE_TOTAL), jnp.float32), (chain, jnp.moveaxis(knot_res, 1, 0)))
    scaled = jnp.einsum('kabv,kbv->kav', dinv_chain, wvalues, precision=highest)

    def retreat(carry, item):
        value = item[1] - jnp.einsum('bav,bv->av', item[0], carry, precision=highest)
        return (value, value)
    _, vvalues = lax.scan(retreat, jnp.zeros((6, VEHICLE_TOTAL), jnp.float32), (chain, scaled), reverse=True)
    land_z = jnp.einsum('abn,bn->an', land_pinv, land_res, precision=highest)
    return (jnp.moveaxis(vvalues, 0, 1), land_z)

def reference(knot_right_side, land_rhs, jac_knot, jac_land, obs_knot, obs_slot, obs_count, send_list, couple, knot_dinv, cuts, land_pinv, knot_damp, land_damp):
    knot_step = jnp.zeros_like(knot_right_side)
    land_step = jnp.zeros_like(land_rhs)
    knot_resid = knot_right_side
    land_resid = land_rhs
    knot_z, land_z = precondition(knot_resid, land_resid, couple, knot_dinv, cuts, land_pinv)
    knot_dir, land_dir = (knot_z, land_z)
    rho = jnp.sum(knot_resid * knot_z) + jnp.sum(land_resid * land_z)
    for turn in range(ITERS):
        knot_q, land_q = hessian_product(knot_dir, land_dir, jac_knot, jac_land, obs_knot, obs_slot, obs_count, send_list, knot_damp, land_damp)
        alpha = rho / (jnp.sum(knot_dir * knot_q) + jnp.sum(land_dir * land_q))
        knot_step = knot_step + alpha * knot_dir
        land_step = land_step + alpha * land_dir
        knot_resid = knot_resid - alpha * knot_q
        land_resid = land_resid - alpha * land_q
        if turn + 1 < ITERS:
            knot_z, land_z = precondition(knot_resid, land_resid, couple, knot_dinv, cuts, land_pinv)
            rho_next = jnp.sum(knot_resid * knot_z) + jnp.sum(land_resid * land_z)
            knot_dir = knot_z + rho_next / rho * knot_dir
            land_dir = land_z + rho_next / rho * land_dir
            rho = rho_next
    return (knot_step, land_step, knot_resid, land_resid)
```

```python
import jax
import jax.numpy as jnp
from jax import lax
from jax.experimental import pallas as pl
from jax.experimental.pallas import tpu as pltpu
from jax.sharding import PartitionSpec as P

f32, bf16, i32 = jnp.float32, jnp.bfloat16, jnp.int32
MESH = pl.DeviceIdType.MESH
NT_DIMS = (((1,), (1,)), ((), ()))
N_TM, N_LM = 16, 8
DEVS = N_TM * N_LM
ITERS = 3
GROUP = 32
OBS = 96


def dot(a, b):
    return jnp.dot(a, b, preferred_element_type=f32)


def dot_nt(a, b):
    return lax.dot_general(a, b, NT_DIMS, preferred_element_type=f32)


def split(x):
    high = x.astype(bf16)
    return high, (x - high.astype(f32)).astype(bf16)


def swap(x):
    return pltpu.roll(x, 64, 1)


def total(x):
    return jnp.sum(jnp.sum(x, axis=0, keepdims=True), axis=1, keepdims=True)


def kernel(
    knot_rhs, land_rhs, jac_knot, jac_land, obs_knot, obs_slot, obs_count, send_list,
    couple, dinv, cuts, pinv, knot_damp, land_damp,
    knot_step, land_step, knot_resid, land_resid,
    jk, jl, obs, live, w_pile, z_pile, u_pile, b_pile, g_nat, u_nat, b_nat, w_row, z_row, knot_z_local, knot_dir,
    land_dir, c_all, a_all, first_all, expanded, land_obs, knot_obs, count_col, knot_hit, knot_hit_t, slot_hit, slot_hit_t,
    pick, pick_t, slots, send_a, recv_a, send_b, recv_b, send_k, recv_k, send_c, recv_c, send_t, recv_t,
    ssem_a, rsem_a, ssem_b, rsem_b, ssem_k, rsem_k, ssem_c, rsem_c, ssem_t, rsem_t, lsem,
):
    me_t, me_l = lax.axis_index("tm"), lax.axis_index("lm")
    me = me_t * N_LM + me_l

    def partner(k):
        d = me + k
        d = jnp.where(d >= DEVS, d - DEVS, d)
        t = lax.div(d, N_LM)
        return d, t, d - t * N_LM

    barrier = pltpu.get_barrier_semaphore()

    def greet(k, carry):
        _, t, l = partner(k)
        pl.semaphore_signal(barrier, inc=1, device_id=(t, l), device_id_type=MESH)
        return carry

    lax.fori_loop(1, DEVS, greet, 0)
    fetch_k = pltpu.make_async_copy(jac_knot, jk, lsem.at[0])
    fetch_l = pltpu.make_async_copy(jac_land, jl, lsem.at[1])
    fetch_k.start()
    fetch_l.start()

    def exchange_all(send, recv, ssem, rsem):
        def to(k):
            d, t, l = partner(k)
            pltpu.make_async_remote_copy(
                send.at[pl.ds(d * 4, 4)], recv.at[pl.ds(me * 4, 4)], ssem, rsem,
                device_id=(t, l), device_id_type=MESH,
            ).start()

        def both(j, carry):
            to(64 + j)
            to(64 - j)
            return carry

        to(64)
        lax.fori_loop(1, 64, both, 0)
        pltpu.make_async_copy(send.at[pl.ds(me * 4, 4)], recv.at[pl.ds(me * 4, 4)], rsem).start()

    def exchange_axis(send, recv, rows, ssem, rsem, over_tm):
        size, mine = (N_TM, me_t) if over_tm else (N_LM, me_l)
        at = recv.at[pl.ds(pl.multiple_of(mine * rows, rows), rows)]

        def to(k, carry):
            d = mine + k
            d = jnp.where(d >= size, d - size, d)
            pltpu.make_async_remote_copy(
                send, at, ssem, rsem,
                device_id=(d, me_l) if over_tm else (me_t, d), device_id_type=MESH,
            ).start()
            return carry

        lax.fori_loop(1, size, to, 0)
        pltpu.make_async_copy(send, at, rsem).start()

    def await_bytes(like, sem):
        pltpu.make_async_copy(like, like, sem).wait()

    lane = lax.broadcasted_iota(i32, (128, 128), 1)
    sub = lax.broadcasted_iota(i32, (128, 128), 0)
    low32 = lax.broadcasted_iota(i32, (32, 128), 1) < 64
    low128 = lane < 64

    def land_apply(r):
        return [pinv[a, 0] * r[0] + pinv[a, 1] * r[1] + pinv[a, 2] * r[2] for a in range(3)]

    def land_inner(x, y):
        s = x[0] * y[0] + x[1] * y[1] + x[2] * y[2]
        return jnp.sum(s, axis=0, keepdims=True)

    def to_all(z, partial, send):
        even = (jnp.where(low32, z[0], swap(z[1])), jnp.where(low32, z[2], 0.0))
        odd = (jnp.where(low32, swap(z[0]), z[1]), jnp.where(low32, swap(z[2]), 0.0))
        tiles = jnp.concatenate(
            [jnp.concatenate(even, axis=1), jnp.concatenate(odd, axis=1)], axis=0
        )
        high, low = split(tiles)
        out = dot(pick[...], jnp.concatenate([high, low], axis=0))
        fill(out, partial, send)

    def fill(out, partial, send):
        extra = jnp.broadcast_to(partial + swap(partial), (128, 128))
        send[pl.ds(0, 128, stride=4), :] = out[:128, :128]
        send[pl.ds(1, 128, stride=4), :] = jnp.where(low128, out[:128, 128:], extra)
        send[pl.ds(2, 128, stride=4), :] = out[128:, :128]
        send[pl.ds(3, 128, stride=4), :] = out[128:, 128:]

    for c in (0, 1):
        wanted = send_list[:, c : c + 1]
        block = 2 * (lane % 32) + lane // 32
        hit = jnp.where((wanted == block) & low128, 1.0, 0.0)
        half = hit[:, :64].astype(bf16)
        pick[c * 128 : (c + 1) * 128, :] = jnp.concatenate([half, half], axis=1)
        hit_t = jnp.transpose(hit)[:64, :].astype(bf16)
        pick_t[:, c * 128 : (c + 1) * 128] = hit_t
        pick_t[:, 256 + c * 128 : 256 + (c + 1) * 128] = hit_t

    land_r = [land_rhs[a] for a in range(3)]
    land_z = land_apply(land_r)
    to_all(land_z, land_inner(land_r, land_z), send_a.at[0])

    open_ends = 1.0 - cuts[...].astype(f32)
    for a in range(6):
        for b in range(6):
            live[(a * 6 + b) * 16 : (a * 6 + b + 1) * 16, :] = couple[a, b] * open_ends
    column = lax.broadcasted_iota(i32, (8, 128), 0)
    unit = tuple(jnp.where(column == a, 1.0, 0.0) for a in range(6))
    none = tuple(jnp.zeros((8, 128), f32) for _ in range(6))

    def live_row(a, b, k):
        return live[pl.ds((a * 6 + b) * 16 + k, 1), :]

    def added(terms):
        terms = list(terms)
        while len(terms) > 1:
            terms = [x + y for x, y in zip(terms[::2], terms[1::2])] + (
                [terms[-1]] if len(terms) % 2 else []
            )
        return terms[0]

    def forward_columns(k, carry):
        at = pl.ds(pl.multiple_of(k * 8, 8), 8)
        value = [carry[a] + jnp.where(column == 6, knot_rhs[a, pl.ds(k, 1), :], 0.0) for a in range(6)]
        for a in range(6):
            w_pile[a, at, :] = value[a]
        return tuple(-added(live_row(a, b, k) * value[b] for b in range(6)) for a in range(6))

    through = lax.fori_loop(0, 16, forward_columns, unit)

    def backward_columns(i, carry):
        k = 15 - i
        at = pl.ds(pl.multiple_of(k * 8, 8), 8)
        z, u, s = carry
        w = [w_pile[b, at, :] for b in range(6)]
        rows = [[live_row(b, a, k) for b in range(6)] for a in range(6)]
        z = tuple(
            added([dinv[a, b, pl.ds(k, 1), :] * w[b] for b in range(6)])
            - added([rows[a][b] * z[b] for b in range(6)])
            for a in range(6)
        )
        u = tuple(
            added([dinv[b, a, pl.ds(k, 1), :] * w[b] for b in range(6)])
            - added([rows[a][b] * u[b] for b in range(6)])
            for a in range(6)
        )
        s = tuple(-added([rows[a][b] * s[b] for b in range(6)]) for a in range(6))
        for a in range(6):
            z_pile[a, at, :] = z[a]
            u_pile[a, at, :] = u[a]
            b_pile[a, at, :] = s[a]
        return z, u, s

    entry, _, _ = lax.fori_loop(0, 16, backward_columns, (none, none, unit))
    for a in range(6):
        send_t[a * 6 : a * 6 + 6, :] = through[a][:6]
        send_t[36 + a * 6 : 36 + a * 6 + 6, :] = entry[a][:6]
        for b in range(6):
            at = slice((a * 6 + b) * 16, (a * 6 + b + 1) * 16)
            g_nat[at, :] = z_pile[a, pl.ds(b, 16, stride=8), :]
            u_nat[at, :] = u_pile[a, pl.ds(b, 16, stride=8), :]
            b_nat[at, :] = b_pile[a, pl.ds(b, 16, stride=8), :]
        knot_z_local[a * 16 : (a + 1) * 16, :] = z_pile[a, pl.ds(6, 16, stride=8), :]

    def block(ref, a, b):
        return ref[(a * 6 + b) * 16 : (a * 6 + b + 1) * 16, :]

    def summary(r):
        return [
            jnp.sum(added([block(ref, b, a) * r[b] for b in range(6)]), axis=0, keepdims=True)
            for ref in (b_nat, u_nat, g_nat)
            for a in range(6)
        ]

    def knot_parts(x):
        return [x[a * 16 : (a + 1) * 16, :] for a in range(6)]

    knot_r = jnp.concatenate([knot_rhs[a] for a in range(6)], axis=0)
    passed_on = summary(knot_parts(knot_r))

    def send_knots(turn, r, parts):
        own = jnp.sum(r * knot_z_local[...], axis=0, keepdims=True)
        for n, row in enumerate(parts + [own]):
            send_c[turn, n : n + 1, :] = row
        for n in range(19, 24):
            send_c[turn, n : n + 1, :] = jnp.zeros((1, 128), f32)
        exchange_axis(send_c.at[turn], recv_c.at[turn], 24, ssem_c.at[turn], rsem_c.at[turn], True)

    pl.semaphore_wait(barrier, DEVS - 1)
    exchange_all(send_a.at[0], recv_a.at[0], ssem_a.at[0], rsem_a.at[0])
    exchange_axis(send_t, recv_t, 72, ssem_t, rsem_t, True)
    send_knots(0, knot_r, passed_on)

    obs[...] = jnp.full((8, 128), -1, i32)
    obs[0:1, 0:OBS] = obs_knot[...]
    obs[1:2, 0:OBS] = obs_slot[...]
    obs[2:3, 0:OBS] = obs_count[...]
    hit_t = jnp.where(obs[0:1, :] == sub // 4, 1.0, 0.0)
    knot_hit_t[...] = jnp.concatenate([hit_t, hit_t], axis=1).astype(bf16)
    knot_hit[...] = jnp.transpose(hit_t).astype(bf16)
    for c in (0, 1):
        hit_t = jnp.where(obs[1:2, :] == 2 * sub + c, 1.0, 0.0)
        slot_hit_t[c * 128 : (c + 1) * 128, :] = jnp.concatenate([hit_t, hit_t], axis=1).astype(bf16)
        slot_hit[:, c * 128 : (c + 1) * 128] = jnp.transpose(hit_t).astype(bf16)
    count_col[...] = jnp.transpose(jnp.broadcast_to(obs[2:3, :].astype(f32), (128, 128)))
    land_obs[...] = jnp.zeros_like(land_obs)
    knot_obs[...] = jnp.zeros_like(knot_obs)
    fetch_k.wait()
    fetch_l.wait()

    def finish_sweeps(turn):
        await_bytes(recv_c.at[turn], rsem_c.at[turn])
        zero = jnp.zeros((1, 128), f32)

        def onward(t, carry):
            c, acc = carry

            def row(n):
                return recv_c[turn, pl.ds(t * 24 + n, 1), :]

            def matrix(n):
                return recv_t[pl.ds(t * 72 + n, 1), :]

            for a in range(6):
                c_all[pl.ds(t * 8 + a, 1), :] = c[a]
                first_all[pl.ds(t * 8 + a, 1), :] = row(6 + a) + added(
                    [matrix(36 + a * 6 + b) * c[b] for b in range(6)]
                )
            acc = acc + row(18) + added([row(12 + a) * c[a] for a in range(6)])
            c = tuple(
                row(a) + added([matrix(a * 6 + b) * c[b] for b in range(6)]) for a in range(6)
            )
            return c, acc

        _, acc = lax.fori_loop(0, N_TM, onward, ((zero,) * 6, zero))

        def back(i, carry):
            t = N_TM - 1 - i
            s, acc = carry
            for a in range(6):
                a_all[pl.ds(t * 8 + a, 1), :] = s[a]
            acc = acc + added([recv_c[turn, pl.ds(t * 24 + a, 1), :] * s[a] for a in range(6)])
            s = tuple(
                first_all[pl.ds(t * 8 + a, 1), :]
                + added([recv_t[pl.ds(t * 72 + b * 6 + a, 1), :] * s[b] for b in range(6)])
                for a in range(6)
            )
            return s, acc

        _, acc = lax.fori_loop(0, N_TM, back, ((zero,) * 6, acc))
        entering = [c_all[pl.ds(me_t * 8 + a, 1), :] for a in range(6)]
        arriving = [a_all[pl.ds(me_t * 8 + a, 1), :] for a in range(6)]
        z = [
            knot_z_local[a * 16 : (a + 1) * 16, :]
            + added([block(g_nat, a, b) * entering[b] for b in range(6)])
            + added([block(b_nat, a, b) * arriving[b] for b in range(6)])
            for a in range(6)
        ]
        return jnp.concatenate(z, axis=0), acc

    def local_sweeps(q):
        w_row[...] = q
        zero = (jnp.zeros((1, 128), f32),) * 6

        def forward(k, carry):
            value = [w_row[pl.ds(a * 16 + k, 1), :] + carry[a] for a in range(6)]
            for a in range(6):
                w_row[pl.ds(a * 16 + k, 1), :] = value[a]
            return tuple(-added([live_row(a, b, k) * value[b] for b in range(6)]) for a in range(6))

        lax.fori_loop(0, 16, forward, zero)
        w = knot_parts(w_row[...])
        for a in range(6):
            z_row[a * 16 : (a + 1) * 16, :] = added([dinv[a, b] * w[b] for b in range(6)])

        def backward(i, carry):
            k = 15 - i
            value = tuple(
                z_row[pl.ds(a * 16 + k, 1), :] - added([live_row(b, a, k) * carry[b] for b in range(6)])
                for a in range(6)
            )
            for a in range(6):
                z_row[pl.ds(a * 16 + k, 1), :] = value[a]
            return value

        lax.fori_loop(0, 16, backward, zero)

    in_block = lax.broadcasted_iota(i32, (GROUP, 32 * GROUP), 1) - 32 * lax.broadcasted_iota(
        i32, (GROUP, 32 * GROUP), 0
    )
    in_block = in_block.astype(f32)
    mod4 = lax.broadcasted_iota(i32, (OBS, 128), 1) % 4

    rho = None
    for turn in range(ITERS):
        knot_z, acc = None, None
        if turn == 0:
            await_bytes(recv_t, rsem_t)
        knot_z, acc = finish_sweeps(turn)
        await_bytes(recv_a.at[turn], rsem_a.at[turn])
        arrived = [recv_a[turn, pl.ds(j, 128, stride=4), :] for j in range(4)]
        rho_next = total(jnp.where(low128, 0.0, arrived[1])) + jnp.sum(acc, axis=1, keepdims=True)
        if turn == 0:
            knot_p = knot_z
            land_p = land_z
        else:
            beta = rho_next / rho
            knot_p = knot_z + beta * knot_dir[...]
            land_p = [land_z[a] + beta * land_dir[a] for a in range(3)]
            arrived = [
                arrived[j] + beta * slots[:, j * 128 : (j + 1) * 128] for j in range(4)
            ]
        rho = rho_next
        knot_dir[...] = knot_p
        for a in range(3):
            land_dir[a] = land_p[a]
        if turn + 1 < ITERS:
            for j in range(4):
                slots[:, j * 128 : (j + 1) * 128] = arrived[j]

        top = jnp.concatenate(arrived[:2], axis=1).astype(bf16)
        bottom = jnp.concatenate(arrived[2:], axis=1).astype(bf16)
        land_in = dot(slot_hit[:OBS, :], jnp.concatenate([top, bottom], axis=0))[:, :192].astype(bf16)
        for i in range(4):
            expanded[pl.ds(i, OBS, stride=4), :] = jnp.where(mod4 == i, knot_p, 0.0)
        knot_in = dot_nt(knot_hit[:OBS, :], expanded[...].astype(bf16)).astype(bf16)
        inner = jnp.zeros((1, 128), f32)
        for g in range(OBS // GROUP):
            at = slice(g * GROUP, (g + 1) * GROUP)
            knot_jac = jk[at].reshape(32 * GROUP, 384)
            land_jac = jl[at].reshape(32 * GROUP, 192)
            sums = dot_nt(knot_in[at, :], knot_jac) + dot_nt(land_in[at, :], land_jac)
            limit = jnp.concatenate([count_col[at, :]] * (GROUP // 4), axis=1)
            sums = jnp.where((in_block >= 0.0) & (in_block < limit), sums, 0.0)
            resid = sums.astype(bf16)
            product = jnp.sum(sums * resid.astype(f32), axis=0, keepdims=True)
            inner = inner + added([product[:, n * 128 : (n + 1) * 128] for n in range(GROUP // 4)])
            land_obs[at, :192] = dot(resid, land_jac)
            knot_obs[at, :] = dot(resid, knot_jac)
        inner = inner + jnp.sum(
            added([land_damp[a] * land_p[a] * land_p[a] for a in range(3)]), axis=0, keepdims=True
        )
        damp = jnp.concatenate([knot_damp[a] for a in range(6)], axis=0)
        inner = inner + (1.0 / N_LM) * jnp.sum(damp * knot_p * knot_p, axis=0, keepdims=True)

        high, low = split(land_obs[...])
        fill(dot(slot_hit_t[...], jnp.concatenate([high, low], axis=0)), inner, send_b.at[turn])
        exchange_all(send_b.at[turn], recv_b.at[turn], ssem_b.at[turn], rsem_b.at[turn])
        high, low = split(knot_obs[...])
        spread = dot(knot_hit_t[...], jnp.concatenate([high, low], axis=0))
        for n in range(3):
            expanded[n * 128 : (n + 1) * 128, :] = jnp.transpose(spread[:, n * 128 : (n + 1) * 128])
        grad = expanded[pl.ds(0, OBS, stride=4), :]
        for i in range(1, 4):
            grad = jnp.where(mod4 == i, expanded[pl.ds(i, OBS, stride=4), :], grad)
        send_k[turn] = grad.astype(bf16)
        exchange_axis(send_k.at[turn], recv_k.at[turn], OBS, ssem_k.at[turn], rsem_k.at[turn], False)

        await_bytes(recv_k.at[turn], rsem_k.at[turn])
        knot_q = added(
            [recv_k[turn, l * OBS : (l + 1) * OBS, :].astype(f32) for l in range(N_LM)]
        ) + damp * knot_p
        if turn + 1 < ITERS:
            local_sweeps(knot_q)
            passed_on_q = summary(knot_parts(knot_q))

        await_bytes(recv_b.at[turn], rsem_b.at[turn])
        back = [recv_b[turn, pl.ds(j, 128, stride=4), :] for j in range(4)]
        alpha = rho / total(jnp.where(low128, 0.0, back[1]))
        knot_r = knot_r - alpha * knot_q
        if turn + 1 < ITERS:
            knot_z_local[...] = knot_z_local[...] - alpha * z_row[...]
            passed_on = [x - alpha * y for x, y in zip(passed_on, passed_on_q)]
            send_knots(turn + 1, knot_r, passed_on)
        pairs = [split(jnp.concatenate(back[2 * c : 2 * c + 2], axis=1)) for c in (0, 1)]
        sums = dot(
            pick_t[...],
            jnp.concatenate([pairs[0][0], pairs[1][0], pairs[0][1], pairs[1][1]], axis=0),
        )
        even, odd = sums[:32], sums[32:]
        land_grad = [
            jnp.where(low32, even[:, :128], swap(odd[:, :128])),
            jnp.where(low32, swap(even[:, :128]), odd[:, :128]),
            jnp.where(low32, even[:, 128:], swap(odd[:, 128:])),
        ]
        land_q = [land_grad[a] + land_damp[a] * land_p[a] for a in range(3)]
        land_r = [land_r[a] - alpha * land_q[a] for a in range(3)]
        if turn + 1 < ITERS:
            land_z = land_apply(land_r)
            to_all(land_z, land_inner(land_r, land_z), send_a.at[turn + 1])
            exchange_all(
                send_a.at[turn + 1], recv_a.at[turn + 1], ssem_a.at[turn + 1], rsem_a.at[turn + 1]
            )
        for a in range(6):
            step = alpha * knot_p[a * 16 : (a + 1) * 16, :]
            knot_step[a] = step if turn == 0 else knot_step[a] + step
        for a in range(3):
            step = alpha * land_p[a]
            land_step[a] = step if turn == 0 else land_step[a] + step
    for a in range(6):
        knot_resid[a] = knot_r[a * 16 : (a + 1) * 16, :]
    for a in range(3):
        land_resid[a] = land_r[a]

    for turn in range(ITERS):
        await_bytes(recv_a.at[turn, pl.ds(0, 4 * (DEVS - 1))], ssem_a.at[turn])
        await_bytes(recv_b.at[turn, pl.ds(0, 4 * (DEVS - 1))], ssem_b.at[turn])
        await_bytes(recv_k.at[turn, pl.ds(0, OBS * (N_LM - 1))], ssem_k.at[turn])
        await_bytes(recv_c.at[turn, pl.ds(0, 24 * (N_TM - 1))], ssem_c.at[turn])
    await_bytes(recv_t.at[pl.ds(0, 72 * (N_TM - 1))], ssem_t)


def on_device(
    knot_right_side, land_rhs, jac_knot, jac_land, obs_knot, obs_slot, obs_count, send_list,
    couple, knot_dinv, cuts, land_pinv, knot_damp, land_damp,
):
    vmem = pl.BlockSpec(memory_space=pltpu.VMEM)
    anywhere = pl.BlockSpec(memory_space=pl.ANY)
    knot = jax.ShapeDtypeStruct((6, 16, 128), f32)
    land = jax.ShapeDtypeStruct((3, 32, 128), f32)
    V = pltpu.VMEM
    dma = pltpu.SemaphoreType.DMA
    outs = pl.pallas_call(
        kernel,
        out_shape=(knot, land, knot, land),
        in_specs=[vmem, vmem, anywhere, anywhere] + [vmem] * 10,
        out_specs=(vmem,) * 4,
        scratch_shapes=[
            V((OBS, 32, 384), bf16),
            V((OBS, 32, 192), bf16),
            V((8, 128), i32),
            V((576, 128), f32),
            V((6, 128, 128), f32),
            V((6, 128, 128), f32),
            V((6, 128, 128), f32),
            V((6, 128, 128), f32),
            V((576, 128), f32),
            V((576, 128), f32),
            V((576, 128), f32),
            V((96, 128), f32),
            V((96, 128), f32),
            V((96, 128), f32),
            V((96, 128), f32),
            V((3, 32, 128), f32),
            V((128, 128), f32),
            V((128, 128), f32),
            V((128, 128), f32),
            V((384, 128), f32),
            V((128, 256), f32),
            V((128, 384), f32),
            V((128, 128), f32),
            V((128, 128), bf16),
            V((128, 256), bf16),
            V((128, 256), bf16),
            V((256, 256), bf16),
            V((256, 128), bf16),
            V((64, 512), bf16),
            V((128, 512), f32),
            V((3, 512, 128), f32),
            V((3, 512, 128), f32),
            V((3, 512, 128), f32),
            V((3, 512, 128), f32),
            V((3, 96, 128), bf16),
            V((3, 768, 128), bf16),
            V((3, 24, 128), f32),
            V((3, 384, 128), f32),
            V((72, 128), f32),
            V((1152, 128), f32),
            dma((3,)), dma((3,)), dma((3,)), dma((3,)), dma((3,)), dma((3,)), dma((3,)), dma((3,)),
            dma, dma, dma((2,)),
        ],
        compiler_params=pltpu.CompilerParams(
            collective_id=0, has_side_effects=True, vmem_limit_bytes=40 * 1024 * 1024
        ),
    )(
        knot_right_side,
        land_rhs.reshape(3, 32, 128),
        jac_knot,
        jac_land,
        obs_knot.reshape(1, OBS),
        obs_slot.reshape(1, OBS),
        obs_count.reshape(1, OBS),
        send_list.reshape(DEVS, 2),
        couple,
        knot_dinv,
        cuts,
        land_pinv.reshape(3, 3, 32, 128),
        knot_damp,
        land_damp.reshape(3, 32, 128),
    )
    return outs[0], outs[1].reshape(3, 4096), outs[2], outs[3].reshape(3, 4096)


def solution(mesh):
    every = ("tm", "lm")
    return jax.shard_map(
        on_device,
        mesh=mesh,
        in_specs=(
            P(None, "tm", None),
            P(None, every),
            P(every, None, None),
            P(every, None, None),
            P(every),
            P(every),
            P(every),
            P(every, None, None),
            P(None, None, "tm", None),
            P(None, None, "tm", None),
            P("tm", None),
            P(None, None, every),
            P(None, "tm", None),
            P(None, every),
        ),
        out_specs=(P(None, "tm", None), P(None, every), P(None, "tm", None), P(None, every)),
        check_vma=False,
    )
```

```python
import jax
import jax.numpy as jnp
from jax import lax
from jax.experimental import pallas as pl
from jax.experimental.pallas import tpu as pltpu
from jax.sharding import PartitionSpec as P

f32, bf16, i32 = jnp.float32, jnp.bfloat16, jnp.int32
MESH = pl.DeviceIdType.MESH
NT_DIMS = (((1,), (1,)), ((), ()))
N_TM, N_LM = 16, 8
DEVS = N_TM * N_LM
ITERS = 3
GROUP = 32
OBS = 96


def dot(a, b):
    return jnp.dot(a, b, preferred_element_type=f32)


def dot_nt(a, b):
    return lax.dot_general(a, b, NT_DIMS, preferred_element_type=f32)


def split(x):
    high = x.astype(bf16)
    return high, (x - high.astype(f32)).astype(bf16)


def swap(x):
    return pltpu.roll(x, 64, 1)


def total(x):
    return jnp.sum(jnp.sum(x, axis=0, keepdims=True), axis=1, keepdims=True)


def kernel(
    *refs,
):
    given, (knot_step, land_step_out, knot_resid, land_resid_out), held = refs[:14], refs[14:18], refs[18:32]
    scratch(given, knot_step, land_step_out, knot_resid, land_resid_out, held, *refs[32:])


def scratch(
    given, knot_step, land_step_out, knot_resid, land_resid_out, held,
    land_rhs, pinv, land_damp, land_step, sums_z, sums_p, obs, live, w_pile, z_pile, u_pile, b_pile, g_nat, u_nat, b_nat, w_row, z_row, knot_z_local, knot_dir,
    land_dir, c_all, a_all, first_all, expanded, land_obs, knot_obs, count_col, knot_hit, knot_hit_t, slot_hit, slot_hit_t,
    pick, pick_t, send_a, recv_a, send_b, recv_b, send_k, recv_k, send_q, recv_q, send_c, recv_c, send_t, recv_t,
    send_z, recv_z, rows_c, rows_t, all_c, change_c, all_t,
    ssem_a, rsem_a, ssem_b, rsem_b, ssem_k, rsem_k, ssem_c, rsem_c, ssem_t, rsem_t, ssem_z, rsem_z, lsem,
):
    me_t, me_l = lax.axis_index("tm"), lax.axis_index("lm")
    me = me_t * N_LM + me_l
    fetches = [pltpu.make_async_copy(x, y, lsem.at[n]) for n, (x, y) in enumerate(zip(given, held))]
    for n in (7, 1, 11, 8, 10, 0, 9, 4, 5, 6, 12, 13, 2, 3):
        fetches[n].start()
    (
        knot_rhs, land_rhs_in, jk, jl, obs_knot, obs_slot, obs_count, send_list,
        couple, dinv, cuts, pinv_in, knot_damp, land_damp_in,
    ) = held

    def partner(k):
        d = me + k
        d = jnp.where(d >= DEVS, d - DEVS, d)
        t = lax.div(d, N_LM)
        return d, t, d - t * N_LM

    barrier = pltpu.get_barrier_semaphore()

    def greet(k, carry):
        _, t, l = partner(k)
        pl.semaphore_signal(barrier, inc=1, device_id=(t, l), device_id_type=MESH)
        return carry

    lax.fori_loop(1, DEVS, greet, 0)

    my_z, my_y = lax.div(me_t, 4), lax.rem(me_t, 4)
    shifts = sorted(
        [(z, y) for z in range(4) for y in range(4)], key=lambda p: -(min(p[0], 4 - p[0]) + min(p[1], 4 - p[1]))
    )

    def wrapped(x, size):
        return jnp.where(x >= size, x - size, x)

    def exchange_all(send, recv, ssem, rsem, part=slice(None)):
        at = recv.at[pl.ds(me * 4, 4)]
        for shift_z, shift_y in shifts[part]:
            t = wrapped(my_z + shift_z, 4) * 4 + wrapped(my_y + shift_y, 4)

            def to(k, carry, t=t):
                l = wrapped(me_l + k, N_LM)
                pltpu.make_async_remote_copy(
                    send.at[pl.ds((t * N_LM + l) * 4, 4)], at, ssem, rsem,
                    device_id=(t, l), device_id_type=MESH,
                ).start()
                return carry

            here = shift_z == 0 and shift_y == 0
            lax.fori_loop(1 if here else 0, N_LM, to, 0)
            if here:
                pltpu.make_async_copy(send.at[pl.ds(me * 4, 4)], at, rsem).start()

    def exchange_axis(send, recv, rows, ssem, rsem, over_tm, scattered=False):
        size, mine = (N_TM, me_t) if over_tm else (N_LM, me_l)
        at = recv.at[pl.ds(pl.multiple_of(mine * rows, rows), rows)]

        def part(d):
            return send.at[pl.ds(pl.multiple_of(d * rows, rows), rows)] if scattered else send

        def to(k, carry):
            d = wrapped(mine + k, size)
            pltpu.make_async_remote_copy(
                part(d), at, ssem, rsem,
                device_id=(d, me_l) if over_tm else (me_t, d), device_id_type=MESH,
            ).start()
            return carry

        lax.fori_loop(1, size, to, 0)
        pltpu.make_async_copy(part(mine), at, rsem).start()

    def await_bytes(like, sem):
        pltpu.make_async_copy(like, like, sem).wait()

    lane = lax.broadcasted_iota(i32, (128, 128), 1)
    sub = lax.broadcasted_iota(i32, (128, 128), 0)
    low32 = lax.broadcasted_iota(i32, (32, 128), 1) < 64
    low128 = lane < 64

    first_lane = me_l * 16

    def packed(ref, rows):
        group = lax.broadcasted_iota(i32, (rows // 8, 128), 1) // 16
        out = jnp.zeros((rows // 8, 128), f32)
        for j in range(8):
            turned = pltpu.roll(ref[pl.ds(j, rows // 8, stride=8), :], wrapped(16 * j + 128 - first_lane, 128), 1)
            out = jnp.where(group == j, turned, out)
        return out

    def unpack(packs, ref):
        rows = packs.shape[0]
        mine = lax.broadcasted_iota(i32, (rows, 128), 1) // 16 == me_l
        for j in range(8):
            turned = pltpu.roll(packs, wrapped(first_lane + 128 - 16 * j, 128), 1)
            ref[pl.ds(j, rows, stride=8), :] = jnp.where(mine, turned, 0.0)

    def land_apply(r):
        return [
            pinv[a, 0:32, :] * r[0] + pinv[a, 32:64, :] * r[1] + pinv[a, 64:96, :] * r[2] for a in range(3)
        ]

    def land_inner(x, y):
        s = x[0] * y[0] + x[1] * y[1] + x[2] * y[2]
        return jnp.sum(s, axis=0, keepdims=True)

    def to_all(z, partial, send):
        even = (jnp.where(low32, z[0], swap(z[1])), jnp.where(low32, z[2], 0.0))
        odd = (jnp.where(low32, swap(z[0]), z[1]), jnp.where(low32, swap(z[2]), 0.0))
        tiles = jnp.concatenate(
            [jnp.concatenate(even, axis=1), jnp.concatenate(odd, axis=1)], axis=0
        )
        high, low = split(tiles)
        out = dot(pick[...], jnp.concatenate([high, low], axis=0))
        fill(out, partial, send)

    def fill(out, partial, send):
        extra = jnp.broadcast_to(partial + swap(partial), (128, 128))
        send[pl.ds(0, 128, stride=4), :] = out[:128, :128]
        send[pl.ds(1, 128, stride=4), :] = jnp.where(low128, out[:128, 128:], extra)
        send[pl.ds(2, 128, stride=4), :] = out[128:, :128]
        send[pl.ds(3, 128, stride=4), :] = out[128:, 128:]

    fetches[7].wait()
    for c in (0, 1):
        code = 2 * (sub % 32) + (sub // 32) % 2
        hit_t = jnp.where(send_list[c : c + 1, :] == code, 1.0, 0.0)
        pick[c * 128 : (c + 1) * 128, :] = jnp.transpose(hit_t).astype(bf16)
        hit_t = hit_t[:64, :].astype(bf16)
        pick_t[:, c * 128 : (c + 1) * 128] = hit_t
        pick_t[:, 256 + c * 128 : 256 + (c + 1) * 128] = hit_t
    fetches[1].wait()
    fetches[11].wait()
    for j in range(32):
        at = slice(j * 128, (j + 1) * 128)
        land_rhs[pl.ds(j, 3, stride=32), :] = land_rhs_in[:, at]
        for a in range(3):
            pinv[a, pl.ds(j, 3, stride=32), :] = pinv_in[a, :, at]

    def land_parts(ref):
        return [ref[a * 32 : (a + 1) * 32, :] for a in range(3)]

    land_r = land_parts(land_rhs)
    land_z = land_apply(land_r)
    to_all(land_z, land_inner(land_r, land_z), send_a.at[0])

    for n in (8, 10, 0, 9):
        fetches[n].wait()
    open_ends = 1.0 - cuts[...].astype(f32)
    for a in range(6):
        for b in range(6):
            live[(a * 6 + b) * 16 : (a * 6 + b + 1) * 16, :] = couple[a, b] * open_ends
    column = lax.broadcasted_iota(i32, (8, 128), 0)
    unit = tuple(jnp.where(column == a, 1.0, 0.0) for a in range(6))
    none = tuple(jnp.zeros((8, 128), f32) for _ in range(6))

    def live_row(a, b, k):
        return live[pl.ds((a * 6 + b) * 16 + k, 1), :]

    def added(terms):
        terms = list(terms)
        while len(terms) > 1:
            terms = [x + y for x, y in zip(terms[::2], terms[1::2])] + (
                [terms[-1]] if len(terms) % 2 else []
            )
        return terms[0]

    def forward_columns(k, carry):
        at = pl.ds(pl.multiple_of(k * 8, 8), 8)
        value = [carry[a] + jnp.where(column == 6, knot_rhs[a, pl.ds(k, 1), :], 0.0) for a in range(6)]
        for a in range(6):
            w_pile[a, at, :] = value[a]
        return tuple(-added(live_row(a, b, k) * value[b] for b in range(6)) for a in range(6))

    through = lax.fori_loop(0, 16, forward_columns, unit)

    def backward_columns(i, carry):
        k = 15 - i
        at = pl.ds(pl.multiple_of(k * 8, 8), 8)
        z, u, s = carry
        w = [w_pile[b, at, :] for b in range(6)]
        rows = [[live_row(b, a, k) for b in range(6)] for a in range(6)]
        z = tuple(
            added([dinv[a, b, pl.ds(k, 1), :] * w[b] for b in range(6)])
            - added([rows[a][b] * z[b] for b in range(6)])
            for a in range(6)
        )
        u = tuple(
            added([dinv[b, a, pl.ds(k, 1), :] * w[b] for b in range(6)])
            - added([rows[a][b] * u[b] for b in range(6)])
            for a in range(6)
        )
        s = tuple(-added([rows[a][b] * s[b] for b in range(6)]) for a in range(6))
        for a in range(6):
            z_pile[a, at, :] = z[a]
            u_pile[a, at, :] = u[a]
            b_pile[a, at, :] = s[a]
        return z, u, s

    entry, _, _ = lax.fori_loop(0, 16, backward_columns, (none, none, unit))
    for a in range(6):
        rows_t[a * 6 : a * 6 + 6, :] = through[a][:6]
        rows_t[36 + a * 6 : 36 + a * 6 + 6, :] = entry[a][:6]
        for b in range(6):
            at = slice((a * 6 + b) * 16, (a * 6 + b + 1) * 16)
            g_nat[at, :] = z_pile[a, pl.ds(b, 16, stride=8), :]
            u_nat[at, :] = u_pile[a, pl.ds(b, 16, stride=8), :]
            b_nat[at, :] = b_pile[a, pl.ds(b, 16, stride=8), :]
        knot_z_local[a * 16 : (a + 1) * 16, :] = z_pile[a, pl.ds(6, 16, stride=8), :]

    def block(ref, a, b):
        return ref[(a * 6 + b) * 16 : (a * 6 + b + 1) * 16, :]

    def summary(r):
        return [
            jnp.sum(added([block(ref, b, a) * r[b] for b in range(6)]), axis=0, keepdims=True)
            for ref in (b_nat, u_nat, g_nat)
            for a in range(6)
        ]

    def knot_parts(x):
        return [x[a * 16 : (a + 1) * 16, :] for a in range(6)]

    knot_r = jnp.concatenate([knot_rhs[a] for a in range(6)], axis=0)
    passed_on = summary(knot_parts(knot_r))

    def send_knots(turn, rows):
        for n, row in enumerate(rows):
            rows_c[n : n + 1, :] = row
        send_c[turn] = packed(rows_c, 24)
        exchange_axis(send_c.at[turn], recv_c.at[turn], 3, ssem_c.at[turn], rsem_c.at[turn], True)

    rows_c[...] = jnp.zeros_like(rows_c)
    send_t[...] = packed(rows_t, 72)
    own = jnp.sum(knot_r * knot_z_local[...], axis=0, keepdims=True)

    pl.semaphore_wait(barrier, DEVS - 1)
    exchange_axis(send_t, recv_t, 9, ssem_t, rsem_t, True)
    send_knots(0, passed_on + [own])
    exchange_all(send_a.at[0], recv_a.at[0], ssem_a.at[0], rsem_a.at[0])

    for n in (4, 5, 6, 12, 13):
        fetches[n].wait()
    for j in range(32):
        land_damp[pl.ds(j, 3, stride=32), :] = land_damp_in[:, j * 128 : (j + 1) * 128]
    obs[...] = jnp.full((8, 128), -1, i32)
    obs[0:1, 0:OBS] = obs_knot[...]
    obs[1:2, 0:OBS] = obs_slot[...]
    obs[2:3, 0:OBS] = obs_count[...]
    hit_t = jnp.where(obs[0:1, :] == sub // 4, 1.0, 0.0)
    knot_hit_t[...] = jnp.concatenate([hit_t, hit_t], axis=1).astype(bf16)
    knot_hit[...] = jnp.transpose(hit_t).astype(bf16)
    for c in (0, 1):
        hit_t = jnp.where(obs[1:2, :] == 2 * sub + c, 1.0, 0.0)
        slot_hit_t[c * 128 : (c + 1) * 128, :] = jnp.concatenate([hit_t, hit_t], axis=1).astype(bf16)
        slot_hit[:, c * 128 : (c + 1) * 128] = jnp.transpose(hit_t).astype(bf16)
    count_col[...] = jnp.transpose(jnp.broadcast_to(obs[2:3, :].astype(f32), (128, 128)))
    land_obs[...] = jnp.zeros_like(land_obs)
    knot_obs[...] = jnp.zeros_like(knot_obs)
    fetches[2].wait()
    fetches[3].wait()

    def finish_sweeps(turn, alpha):
        await_bytes(recv_c.at[turn], rsem_c.at[turn])
        if turn == 0:
            unpack(recv_c[turn], all_c)
        else:
            unpack(recv_c[turn], change_c)
            bends = change_c[pl.ds(19, N_TM, stride=24), :]
            all_c[...] = all_c[...] - alpha * change_c[...]
            all_c[pl.ds(18, N_TM, stride=24), :] = all_c[pl.ds(18, N_TM, stride=24), :] + alpha * alpha * bends
        zero = jnp.zeros((1, 128), f32)

        def onward(t, carry):
            c, acc = carry

            def row(n):
                return all_c[pl.ds(t * 24 + n, 1), :]

            def matrix(n):
                return all_t[pl.ds(t * 72 + n, 1), :]

            for a in range(6):
                c_all[pl.ds(t * 8 + a, 1), :] = c[a]
                first_all[pl.ds(t * 8 + a, 1), :] = row(6 + a) + added(
                    [matrix(36 + a * 6 + b) * c[b] for b in range(6)]
                )
            acc = acc + row(18) + added([row(12 + a) * c[a] for a in range(6)])
            c = tuple(
                row(a) + added([matrix(a * 6 + b) * c[b] for b in range(6)]) for a in range(6)
            )
            return c, acc

        _, acc = lax.fori_loop(0, N_TM, onward, ((zero,) * 6, zero))

        def back(i, carry):
            t = N_TM - 1 - i
            s, acc = carry
            for a in range(6):
                a_all[pl.ds(t * 8 + a, 1), :] = s[a]
            acc = acc + added([all_c[pl.ds(t * 24 + a, 1), :] * s[a] for a in range(6)])
            s = tuple(
                first_all[pl.ds(t * 8 + a, 1), :]
                + added([all_t[pl.ds(t * 72 + b * 6 + a, 1), :] * s[b] for b in range(6)])
                for a in range(6)
            )
            return s, acc

        _, acc = lax.fori_loop(0, N_TM, back, ((zero,) * 6, acc))
        entering = [c_all[pl.ds(me_t * 8 + a, 1), :] for a in range(6)]
        arriving = [a_all[pl.ds(me_t * 8 + a, 1), :] for a in range(6)]
        z = [
            knot_z_local[a * 16 : (a + 1) * 16, :]
            + added([block(g_nat, a, b) * entering[b] for b in range(6)])
            + added([block(b_nat, a, b) * arriving[b] for b in range(6)])
            for a in range(6)
        ]
        return jnp.concatenate(z, axis=0), acc

    def local_sweeps(q):
        w_row[...] = q
        zero = (jnp.zeros((1, 128), f32),) * 6

        def forward(k, carry):
            value = [w_row[pl.ds(a * 16 + k, 1), :] + carry[a] for a in range(6)]
            for a in range(6):
                w_row[pl.ds(a * 16 + k, 1), :] = value[a]
            return tuple(-added([live_row(a, b, k) * value[b] for b in range(6)]) for a in range(6))

        lax.fori_loop(0, 16, forward, zero)
        w = knot_parts(w_row[...])
        for a in range(6):
            z_row[a * 16 : (a + 1) * 16, :] = added([dinv[a, b] * w[b] for b in range(6)])

        def backward(i, carry):
            k = 15 - i
            value = tuple(
                z_row[pl.ds(a * 16 + k, 1), :] - added([live_row(b, a, k) * carry[b] for b in range(6)])
                for a in range(6)
            )
            for a in range(6):
                z_row[pl.ds(a * 16 + k, 1), :] = value[a]
            return value

        lax.fori_loop(0, 16, backward, zero)

    in_block = lax.broadcasted_iota(i32, (GROUP, 32 * GROUP), 1) - 32 * lax.broadcasted_iota(
        i32, (GROUP, 32 * GROUP), 0
    )
    in_block = in_block.astype(f32)
    mod4 = lax.broadcasted_iota(i32, (OBS, 128), 1) % 4

    land_damps = land_parts(land_damp)
    rho, alpha = None, None
    for turn in range(ITERS):
        if turn == 0:
            await_bytes(recv_t, rsem_t)
            unpack(recv_t[...], all_t)
        knot_z, acc = finish_sweeps(turn, alpha)
        last = turn + 1 == ITERS
        filler = jnp.zeros((31, 128), f32)
        expanded[:128, :] = jnp.transpose(jnp.concatenate([knot_z, acc, filler], axis=0))
        mine = pl.ds(pl.multiple_of(first_lane, 16), 16)
        send_z[turn, :16, :] = expanded[mine, :]
        height = 16
        if last:
            height = 32
            expanded[128:256, :] = jnp.transpose(jnp.concatenate([knot_r, acc, filler], axis=0))
            send_z[turn, 16:, :] = expanded[pl.ds(pl.multiple_of(first_lane + 128, 16), 16), :]
        from_z = recv_z.at[turn, pl.ds(0, N_LM * height)]
        exchange_axis(
            send_z.at[turn, pl.ds(0, height)], from_z, height, ssem_z.at[turn], rsem_z.at[turn], False
        )
        await_bytes(from_z, rsem_z.at[turn])

        def gathered(first):
            return jnp.transpose(
                jnp.concatenate(
                    [recv_z[turn, l * height + first : l * height + first + 16, :] for l in range(N_LM)], axis=0
                )
            )

        knot_z = gathered(0)
        acc, knot_z = knot_z[96:97, :], knot_z[:96, :]
        if last:
            knot_r = gathered(16)[:96, :]

        for i in range(4):
            expanded[pl.ds(i, OBS, stride=4), :] = jnp.where(mod4 == i, knot_z, 0.0)
        knot_in = [dot_nt(knot_hit[:OBS, :], x).astype(bf16) for x in split(expanded[...])]
        for g in range(OBS // GROUP):
            at = slice(g * GROUP, (g + 1) * GROUP)
            both = dot_nt(
                jnp.concatenate([x[at, :] for x in knot_in], axis=0), jk[at].reshape(32 * GROUP, 384)
            )
            sums_z[at, :] = both[:GROUP] + both[GROUP:]

        await_bytes(recv_a.at[turn], rsem_a.at[turn])
        arrived = [recv_a[turn, pl.ds(j, 128, stride=4), :] for j in range(4)]
        top = jnp.concatenate(arrived[:2], axis=1)
        bottom = jnp.concatenate(arrived[2:], axis=1)
        land_in = [
            dot(slot_hit[:OBS, :], x)[:, :192].astype(bf16)
            for x in split(jnp.concatenate([top, bottom], axis=0))
        ]
        rho_next = total(jnp.where(low128, 0.0, arrived[1])) + jnp.sum(acc, axis=1, keepdims=True)
        if turn == 0:
            knot_p = knot_z
            land_p = land_z
        else:
            beta = rho_next / rho
            knot_p = knot_z + beta * knot_dir[...]
            land_p = [land_z[a] + beta * land_dir[a] for a in range(3)]
        rho = rho_next
        knot_dir[...] = knot_p
        for a in range(3):
            land_dir[a] = land_p[a]
        inner = jnp.zeros((1, 128), f32)
        resids = []
        for g in range(OBS // GROUP):
            at = slice(g * GROUP, (g + 1) * GROUP)
            land_jac = jl[at].reshape(32 * GROUP, 192)
            both = dot_nt(jnp.concatenate([x[at, :] for x in land_in], axis=0), land_jac)
            sums = sums_z[at, :] + (both[:GROUP] + both[GROUP:])
            if turn > 0:
                sums = sums + beta * sums_p[at, :]
            if turn + 1 < ITERS:
                sums_p[at, :] = sums
            limit = jnp.concatenate([count_col[at, :]] * (GROUP // 4), axis=1)
            sums = jnp.where((in_block >= 0.0) & (in_block < limit), sums, 0.0)
            resid = sums.astype(bf16)
            product = jnp.sum(sums * resid.astype(f32), axis=0, keepdims=True)
            inner = inner + added([product[:, n * 128 : (n + 1) * 128] for n in range(GROUP // 4)])
            resids.append(resid)
            land_obs[at, :192] = dot(resid, land_jac)
        inner = inner + jnp.sum(
            added([land_damps[a] * land_p[a] * land_p[a] for a in range(3)]), axis=0, keepdims=True
        )
        damp = jnp.concatenate([knot_damp[a] for a in range(6)], axis=0)
        inner = inner + (1.0 / N_LM) * jnp.sum(damp * knot_p * knot_p, axis=0, keepdims=True)

        high, low = split(land_obs[...])
        fill(dot(slot_hit_t[...], jnp.concatenate([high, low], axis=0)), inner, send_b.at[turn])
        far, near = slice(0, 8), slice(8, 16)
        exchange_all(send_b.at[turn], recv_b.at[turn], ssem_b.at[turn], rsem_b.at[turn], far)
        for g in range(OBS // GROUP):
            at = slice(g * GROUP, (g + 1) * GROUP)
            knot_obs[at, :] = dot(resids[g], jk[at].reshape(32 * GROUP, 384))
        high, low = split(knot_obs[...])
        spread = dot(knot_hit_t[...], jnp.concatenate([high, low], axis=0))
        for n in range(3):
            expanded[n * 128 : (n + 1) * 128, :] = jnp.transpose(spread[:, n * 128 : (n + 1) * 128])
        grad = expanded[pl.ds(0, OBS, stride=4), :]
        for i in range(1, 4):
            grad = jnp.where(mod4 == i, expanded[pl.ds(i, OBS, stride=4), :], grad)
        if last:
            send_k[...] = grad.astype(bf16)
            exchange_axis(send_k, recv_k, OBS, ssem_k.at[turn], rsem_k.at[turn], False)
        else:
            send_q[turn] = jnp.transpose(
                jnp.concatenate([grad, jnp.zeros((32, 128), f32)], axis=0)
            ).astype(bf16)
            exchange_axis(
                send_q.at[turn], recv_q.at[turn], 16, ssem_k.at[turn], rsem_k.at[turn], False, True
            )
        exchange_all(send_b.at[turn], recv_b.at[turn], ssem_b.at[turn], rsem_b.at[turn], near)

        if last:
            await_bytes(recv_k, rsem_k.at[turn])
            knot_q = added([recv_k[l * OBS : (l + 1) * OBS, :].astype(f32) for l in range(N_LM)])
            knot_q = knot_q + damp * knot_p
        else:
            await_bytes(recv_q.at[turn], rsem_k.at[turn])
            expanded[:128, :] = jnp.zeros((128, 128), f32)
            expanded[mine, :] = added(
                [recv_q[turn, l * 16 : (l + 1) * 16, :].astype(f32) for l in range(N_LM)]
            )
            knot_q = jnp.transpose(expanded[:128, :])[:96, :] + damp * knot_p
            local_sweeps(knot_q)
            answers = z_row[...]
            slope = knot_q * knot_z_local[...] + knot_r * answers
            send_knots(
                turn + 1,
                summary(knot_parts(knot_q))
                + [jnp.sum(x, axis=0, keepdims=True) for x in (slope, knot_q * answers)],
            )

        await_bytes(recv_b.at[turn], rsem_b.at[turn])
        back = [recv_b[turn, pl.ds(j, 128, stride=4), :] for j in range(4)]
        alpha = rho / total(jnp.where(low128, 0.0, back[1]))
        knot_r = knot_r - alpha * knot_q
        if turn + 1 < ITERS:
            knot_z_local[...] = knot_z_local[...] - alpha * z_row[...]
        pairs = [split(jnp.concatenate(back[2 * c : 2 * c + 2], axis=1)) for c in (0, 1)]
        sums = dot(
            pick_t[...],
            jnp.concatenate([pairs[0][0], pairs[1][0], pairs[0][1], pairs[1][1]], axis=0),
        )
        even, odd = sums[:32], sums[32:]
        land_grad = [
            jnp.where(low32, even[:, :128], swap(odd[:, :128])),
            jnp.where(low32, swap(even[:, :128]), odd[:, :128]),
            jnp.where(low32, even[:, 128:], swap(odd[:, 128:])),
        ]
        land_q = [land_grad[a] + land_damps[a] * land_p[a] for a in range(3)]
        land_r = [land_r[a] - alpha * land_q[a] for a in range(3)]
        if turn + 1 < ITERS:
            land_z = land_apply(land_r)
            to_all(land_z, land_inner(land_r, land_z), send_a.at[turn + 1])
            exchange_all(
                send_a.at[turn + 1], recv_a.at[turn + 1], ssem_a.at[turn + 1], rsem_a.at[turn + 1]
            )
        for a in range(6):
            step = alpha * knot_p[a * 16 : (a + 1) * 16, :]
            knot_step[a] = step if turn == 0 else knot_step[a] + step
        for a in range(3):
            at = slice(a * 32, (a + 1) * 32)
            step = alpha * land_p[a]
            land_step[at, :] = step if turn == 0 else land_step[at, :] + step
    for a in range(6):
        knot_resid[a] = knot_r[a * 16 : (a + 1) * 16, :]
    for a in range(3):
        land_rhs[a * 32 : (a + 1) * 32, :] = land_r[a]
    for j in range(32):
        at = slice(j * 128, (j + 1) * 128)
        land_step_out[:, at] = land_step[pl.ds(j, 3, stride=32), :]
        land_resid_out[:, at] = land_rhs[pl.ds(j, 3, stride=32), :]

    for turn in range(ITERS):
        await_bytes(recv_a.at[turn, pl.ds(0, 4 * (DEVS - 1))], ssem_a.at[turn])
        await_bytes(recv_b.at[turn, pl.ds(0, 4 * (DEVS - 1))], ssem_b.at[turn])
        await_bytes(recv_c.at[turn, pl.ds(0, 3 * (N_TM - 1))], ssem_c.at[turn])
        height = 32 if turn + 1 == ITERS else 16
        await_bytes(recv_z.at[turn, pl.ds(0, height * (N_LM - 1))], ssem_z.at[turn])
        if turn + 1 < ITERS:
            await_bytes(recv_q.at[turn, pl.ds(0, 16 * (N_LM - 1))], ssem_k.at[turn])
    await_bytes(recv_k.at[pl.ds(0, OBS * (N_LM - 1))], ssem_k.at[ITERS - 1])
    await_bytes(recv_t.at[pl.ds(0, 9 * (N_TM - 1))], ssem_t)


def on_device(
    knot_right_side, land_rhs, jac_knot, jac_land, obs_knot, obs_slot, obs_count, send_list,
    couple, knot_dinv, cuts, land_pinv, knot_damp, land_damp,
):
    vmem = pl.BlockSpec(memory_space=pltpu.VMEM)
    outside = pl.BlockSpec(memory_space=pltpu.HBM)
    knot = jax.ShapeDtypeStruct((6, 16, 128), f32)
    land = jax.ShapeDtypeStruct((3, 4096), f32)
    V = pltpu.VMEM
    dma = pltpu.SemaphoreType.DMA
    outs = pl.pallas_call(
        kernel,
        out_shape=(knot, land, knot, land),
        in_specs=[outside] * 14,
        out_specs=(vmem,) * 4,
        scratch_shapes=[
            V((6, 16, 128), f32),
            V((3, 4096), f32),
            V((OBS, 32, 384), bf16),
            V((OBS, 32, 192), bf16),
            V((1, OBS), i32),
            V((1, OBS), i32),
            V((1, OBS), i32),
            V((2, DEVS), i32),
            V((6, 6, 16, 128), f32),
            V((6, 6, 16, 128), f32),
            V((16, 128), i32),
            V((3, 3, 4096), f32),
            V((6, 16, 128), f32),
            V((3, 4096), f32),
            V((96, 128), f32),
            V((3, 96, 128), f32),
            V((96, 128), f32),
            V((96, 128), f32),
            V((OBS, 32 * GROUP), f32),
            V((OBS, 32 * GROUP), f32),
            V((8, 128), i32),
            V((576, 128), f32),
            V((6, 128, 128), f32),
            V((6, 128, 128), f32),
            V((6, 128, 128), f32),
            V((6, 128, 128), f32),
            V((576, 128), f32),
            V((576, 128), f32),
            V((576, 128), f32),
            V((96, 128), f32),
            V((96, 128), f32),
            V((96, 128), f32),
            V((96, 128), f32),
            V((3, 32, 128), f32),
            V((128, 128), f32),
            V((128, 128), f32),
            V((128, 128), f32),
            V((384, 128), f32),
            V((128, 256), f32),
            V((128, 384), f32),
            V((128, 128), f32),
            V((128, 128), bf16),
            V((128, 256), bf16),
            V((128, 256), bf16),
            V((256, 256), bf16),
            V((256, 128), bf16),
            V((64, 512), bf16),
            V((3, 512, 128), f32),
            V((3, 512, 128), f32),
            V((3, 512, 128), f32),
            V((3, 512, 128), f32),
            V((96, 128), bf16),
            V((768, 128), bf16),
            V((2, 128, 128), bf16),
            V((2, 128, 128), bf16),
            V((3, 3, 128), f32),
            V((3, 48, 128), f32),
            V((9, 128), f32),
            V((144, 128), f32),
            V((3, 32, 128), f32),
            V((3, 256, 128), f32),
            V((24, 128), f32),
            V((72, 128), f32),
            V((384, 128), f32),
            V((384, 128), f32),
            V((1152, 128), f32),
            dma((3,)), dma((3,)), dma((3,)), dma((3,)), dma((3,)), dma((3,)), dma((3,)), dma((3,)),
            dma, dma, dma((3,)), dma((3,)), dma((14,)),
        ],
        compiler_params=pltpu.CompilerParams(
            collective_id=0, has_side_effects=True, vmem_limit_bytes=60 * 1024 * 1024
        ),
    )(
        knot_right_side,
        land_rhs,
        jac_knot,
        jac_land,
        obs_knot.reshape(1, OBS),
        obs_slot.reshape(1, OBS),
        obs_count.reshape(1, OBS),
        send_list.reshape(DEVS, 2).T,
        couple,
        knot_dinv,
        cuts,
        land_pinv,
        knot_damp,
        land_damp,
    )
    return outs


def solution(mesh):
    every = ("tm", "lm")
    return jax.shard_map(
        on_device,
        mesh=mesh,
        in_specs=(
            P(None, "tm", None),
            P(None, every),
            P(every, None, None),
            P(every, None, None),
            P(every),
            P(every),
            P(every),
            P(every, None, None),
            P(None, None, "tm", None),
            P(None, None, "tm", None),
            P("tm", None),
            P(None, None, every),
            P(None, "tm", None),
            P(None, every),
        ),
        out_specs=(P(None, "tm", None), P(None, every), P(None, "tm", None), P(None, every)),
        check_vma=False,
    )
```

```python
import jax
import jax.numpy as jnp
from jax import lax
from jax.experimental import pallas as pl
from jax.experimental.pallas import tpu as pltpu
from jax.sharding import PartitionSpec as P

f32, bf16, i32 = jnp.float32, jnp.bfloat16, jnp.int32
MESH = pl.DeviceIdType.MESH
NT_DIMS = (((1,), (1,)), ((), ()))
N_TM, N_LM = 16, 8
DEVS = N_TM * N_LM
ITERS = 3
GROUP = 32
OBS = 96


def dot(a, b):
    return jnp.dot(a, b, preferred_element_type=f32)


def dot_nt(a, b):
    return lax.dot_general(a, b, NT_DIMS, preferred_element_type=f32)


def split(x):
    high = x.astype(bf16)
    return high, (x - high.astype(f32)).astype(bf16)


def swap(x):
    return pltpu.roll(x, 64, 1)


def total(x):
    return jnp.sum(jnp.sum(x, axis=0, keepdims=True), axis=1, keepdims=True)


def kernel(
    *refs,
):
    given, (knot_step, land_step_out, knot_resid, land_resid_out), held = refs[:14], refs[14:18], refs[18:32]
    scratch(given, knot_step, land_step_out, knot_resid, land_resid_out, held, *refs[32:])


def scratch(
    given, knot_step, land_step_out, knot_resid, land_resid_out, held,
    land_rhs, pinv, land_damp, land_step, sums_z, sums_p, obs, live, w_pile, z_pile, u_pile, b_pile, g_nat, u_nat, b_nat, w_row, z_row, knot_z_local, knot_dir,
    land_dir, c_all, a_all, first_all, expanded, land_obs, knot_obs, count_col, knot_hit, knot_hit_t, slot_hit, slot_hit_t,
    pick, pick_t, send_a, recv_a, send_b, recv_b, send_k, recv_k, send_q, recv_q, send_c, recv_c, send_t, recv_t,
    send_z, recv_z, rows_c, rows_t, all_c, change_c, all_t,
    ssem_a, rsem_a, ssem_b, rsem_b, ssem_k, rsem_k, ssem_c, rsem_c, ssem_t, rsem_t, ssem_z, rsem_z, lsem,
):
    me_t, me_l = lax.axis_index("tm"), lax.axis_index("lm")
    me = me_t * N_LM + me_l
    fetches = [pltpu.make_async_copy(x, y, lsem.at[n]) for n, (x, y) in enumerate(zip(given, held))]
    (
        knot_rhs, land_rhs_in, jk, jl, obs_knot, obs_slot, obs_count, send_list,
        couple, dinv, cuts, pinv_in, knot_damp, land_damp_in,
    ) = held

    my_z, my_y = lax.div(me_t, 4), lax.rem(me_t, 4)
    shifts = sorted(
        [(z, y) for z in range(4) for y in range(4)], key=lambda p: -(min(p[0], 4 - p[0]) + min(p[1], 4 - p[1]))
    )

    def wrapped(x, size):
        return jnp.where(x >= size, x - size, x)

    barrier = pltpu.get_barrier_semaphore()
    for shift_z, shift_y in shifts:
        greeted = wrapped(my_z + shift_z, 4) * 4 + wrapped(my_y + shift_y, 4)

        def greet(k, carry, t=greeted):
            pl.semaphore_signal(
                barrier, inc=1, device_id=(t, wrapped(me_l + k, N_LM)), device_id_type=MESH
            )
            return carry

        lax.fori_loop(1 if shift_z == 0 and shift_y == 0 else 0, N_LM, greet, 0)

    for n in (7, 1, 11, 8, 10, 0, 9, 4, 5, 6, 12, 13, 2, 3):
        fetches[n].start()

    def exchange_all(send, recv, ssem, rsem, part=slice(None)):
        at = recv.at[pl.ds(me * 4, 4)]
        for shift_z, shift_y in shifts[part]:
            t = wrapped(my_z + shift_z, 4) * 4 + wrapped(my_y + shift_y, 4)

            def to(k, carry, t=t):
                l = wrapped(me_l + k, N_LM)
                pltpu.make_async_remote_copy(
                    send.at[pl.ds((t * N_LM + l) * 4, 4)], at, ssem, rsem,
                    device_id=(t, l), device_id_type=MESH,
                ).start()
                return carry

            here = shift_z == 0 and shift_y == 0
            lax.fori_loop(1 if here else 0, N_LM, to, 0)
            if here:
                pltpu.make_async_copy(send.at[pl.ds(me * 4, 4)], at, rsem).start()

    def exchange_axis(send, recv, rows, ssem, rsem, over_tm, scattered=False):
        size, mine = (N_TM, me_t) if over_tm else (N_LM, me_l)
        at = recv.at[pl.ds(pl.multiple_of(mine * rows, rows), rows)]

        def part(d):
            return send.at[pl.ds(pl.multiple_of(d * rows, rows), rows)] if scattered else send

        def to(k, carry):
            d = wrapped(mine + k, size)
            pltpu.make_async_remote_copy(
                part(d), at, ssem, rsem,
                device_id=(d, me_l) if over_tm else (me_t, d), device_id_type=MESH,
            ).start()
            return carry

        lax.fori_loop(1, size, to, 0)
        pltpu.make_async_copy(part(mine), at, rsem).start()

    def await_bytes(like, sem):
        pltpu.make_async_copy(like, like, sem).wait()

    lane = lax.broadcasted_iota(i32, (128, 128), 1)
    sub = lax.broadcasted_iota(i32, (128, 128), 0)
    low32 = lax.broadcasted_iota(i32, (32, 128), 1) < 64
    low128 = lane < 64

    first_lane = me_l * 16

    def packed(ref, rows):
        group = lax.broadcasted_iota(i32, (rows // 8, 128), 1) // 16
        out = jnp.zeros((rows // 8, 128), f32)
        for j in range(8):
            turned = pltpu.roll(ref[pl.ds(j, rows // 8, stride=8), :], wrapped(16 * j + 128 - first_lane, 128), 1)
            out = jnp.where(group == j, turned, out)
        return out

    def unpack(packs, ref):
        rows = packs.shape[0]
        mine = lax.broadcasted_iota(i32, (rows, 128), 1) // 16 == me_l
        for j in range(8):
            turned = pltpu.roll(packs, wrapped(first_lane + 128 - 16 * j, 128), 1)
            ref[pl.ds(j, rows, stride=8), :] = jnp.where(mine, turned, 0.0)

    def land_apply(r):
        return [
            pinv[a, 0:32, :] * r[0] + pinv[a, 32:64, :] * r[1] + pinv[a, 64:96, :] * r[2] for a in range(3)
        ]

    def land_inner(x, y):
        s = x[0] * y[0] + x[1] * y[1] + x[2] * y[2]
        return jnp.sum(s, axis=0, keepdims=True)

    def to_all(z, partial, send):
        even = (jnp.where(low32, z[0], swap(z[1])), jnp.where(low32, z[2], 0.0))
        odd = (jnp.where(low32, swap(z[0]), z[1]), jnp.where(low32, swap(z[2]), 0.0))
        tiles = jnp.concatenate(
            [jnp.concatenate(even, axis=1), jnp.concatenate(odd, axis=1)], axis=0
        )
        high, low = split(tiles)
        out = dot(pick[...], jnp.concatenate([high, low], axis=0))
        fill(out, partial, send)

    def fill(out, partial, send):
        extra = jnp.broadcast_to(partial + swap(partial), (128, 128))
        send[pl.ds(0, 128, stride=4), :] = out[:128, :128]
        send[pl.ds(1, 128, stride=4), :] = jnp.where(low128, out[:128, 128:], extra)
        send[pl.ds(2, 128, stride=4), :] = out[128:, :128]
        send[pl.ds(3, 128, stride=4), :] = out[128:, 128:]

    fetches[7].wait()
    for c in (0, 1):
        code = 2 * (sub % 32) + (sub // 32) % 2
        hit_t = jnp.where(send_list[c : c + 1, :] == code, 1.0, 0.0)
        pick[c * 128 : (c + 1) * 128, :] = jnp.transpose(hit_t).astype(bf16)
        hit_t = hit_t[:64, :].astype(bf16)
        pick_t[:, c * 128 : (c + 1) * 128] = hit_t
        pick_t[:, 256 + c * 128 : 256 + (c + 1) * 128] = hit_t
    fetches[1].wait()
    fetches[11].wait()
    for j in range(32):
        at = slice(j * 128, (j + 1) * 128)
        land_rhs[pl.ds(j, 3, stride=32), :] = land_rhs_in[:, at]
        for a in range(3):
            pinv[a, pl.ds(j, 3, stride=32), :] = pinv_in[a, :, at]

    def land_parts(ref):
        return [ref[a * 32 : (a + 1) * 32, :] for a in range(3)]

    land_r = land_parts(land_rhs)
    land_z = land_apply(land_r)
    to_all(land_z, land_inner(land_r, land_z), send_a.at[0])

    for n in (8, 10, 0, 9):
        fetches[n].wait()
    open_ends = 1.0 - cuts[...].astype(f32)
    for a in range(6):
        for b in range(6):
            live[(a * 6 + b) * 16 : (a * 6 + b + 1) * 16, :] = couple[a, b] * open_ends
    column = lax.broadcasted_iota(i32, (8, 128), 0)
    unit = tuple(jnp.where(column == a, 1.0, 0.0) for a in range(6))
    none = tuple(jnp.zeros((8, 128), f32) for _ in range(6))

    def live_row(a, b, k):
        return live[pl.ds((a * 6 + b) * 16 + k, 1), :]

    def added(terms):
        terms = list(terms)
        while len(terms) > 1:
            terms = [x + y for x, y in zip(terms[::2], terms[1::2])] + (
                [terms[-1]] if len(terms) % 2 else []
            )
        return terms[0]

    def forward_columns(k, carry):
        at = pl.ds(pl.multiple_of(k * 8, 8), 8)
        value = [carry[a] + jnp.where(column == 6, knot_rhs[a, pl.ds(k, 1), :], 0.0) for a in range(6)]
        for a in range(6):
            w_pile[a, at, :] = value[a]
        return tuple(-added(live_row(a, b, k) * value[b] for b in range(6)) for a in range(6))

    through = lax.fori_loop(0, 16, forward_columns, unit)

    def backward_columns(i, carry):
        k = 15 - i
        at = pl.ds(pl.multiple_of(k * 8, 8), 8)
        z, u, s = carry
        w = [w_pile[b, at, :] for b in range(6)]
        rows = [[live_row(b, a, k) for b in range(6)] for a in range(6)]
        z = tuple(
            added([dinv[a, b, pl.ds(k, 1), :] * w[b] for b in range(6)])
            - added([rows[a][b] * z[b] for b in range(6)])
            for a in range(6)
        )
        u = tuple(
            added([dinv[b, a, pl.ds(k, 1), :] * w[b] for b in range(6)])
            - added([rows[a][b] * u[b] for b in range(6)])
            for a in range(6)
        )
        s = tuple(-added([rows[a][b] * s[b] for b in range(6)]) for a in range(6))
        for a in range(6):
            z_pile[a, at, :] = z[a]
            u_pile[a, at, :] = u[a]
            b_pile[a, at, :] = s[a]
        return z, u, s

    entry, _, _ = lax.fori_loop(0, 16, backward_columns, (none, none, unit))
    for a in range(6):
        rows_t[a * 6 : a * 6 + 6, :] = through[a][:6]
        rows_t[36 + a * 6 : 36 + a * 6 + 6, :] = entry[a][:6]
        for b in range(6):
            at = slice((a * 6 + b) * 16, (a * 6 + b + 1) * 16)
            g_nat[at, :] = z_pile[a, pl.ds(b, 16, stride=8), :]
            u_nat[at, :] = u_pile[a, pl.ds(b, 16, stride=8), :]
            b_nat[at, :] = b_pile[a, pl.ds(b, 16, stride=8), :]
        knot_z_local[a * 16 : (a + 1) * 16, :] = z_pile[a, pl.ds(6, 16, stride=8), :]

    def block(ref, a, b):
        return ref[(a * 6 + b) * 16 : (a * 6 + b + 1) * 16, :]

    def summary(r):
        return [
            jnp.sum(added([block(ref, b, a) * r[b] for b in range(6)]), axis=0, keepdims=True)
            for ref in (b_nat, u_nat, g_nat)
            for a in range(6)
        ]

    def knot_parts(x):
        return [x[a * 16 : (a + 1) * 16, :] for a in range(6)]

    knot_r = jnp.concatenate([knot_rhs[a] for a in range(6)], axis=0)
    passed_on = summary(knot_parts(knot_r))

    def send_knots(turn, rows):
        for n, row in enumerate(rows):
            rows_c[n : n + 1, :] = row
        send_c[turn] = packed(rows_c, 24)
        exchange_axis(send_c.at[turn], recv_c.at[turn], 3, ssem_c.at[turn], rsem_c.at[turn], True)

    rows_c[...] = jnp.zeros_like(rows_c)
    send_t[...] = packed(rows_t, 72)
    own = jnp.sum(knot_r * knot_z_local[...], axis=0, keepdims=True)

    pl.semaphore_wait(barrier, DEVS - 1)
    exchange_axis(send_t, recv_t, 9, ssem_t, rsem_t, True)
    send_knots(0, passed_on + [own])
    exchange_all(send_a.at[0], recv_a.at[0], ssem_a.at[0], rsem_a.at[0])

    for n in (4, 5, 6, 12, 13):
        fetches[n].wait()
    for j in range(32):
        land_damp[pl.ds(j, 3, stride=32), :] = land_damp_in[:, j * 128 : (j + 1) * 128]
    obs[...] = jnp.full((8, 128), -1, i32)
    obs[0:1, 0:OBS] = obs_knot[...]
    obs[1:2, 0:OBS] = obs_slot[...]
    obs[2:3, 0:OBS] = obs_count[...]
    hit_t = jnp.where(obs[0:1, :] == sub // 4, 1.0, 0.0)
    knot_hit_t[...] = jnp.concatenate([hit_t, hit_t], axis=1).astype(bf16)
    knot_hit[...] = jnp.transpose(hit_t).astype(bf16)
    for c in (0, 1):
        hit_t = jnp.where(obs[1:2, :] == 2 * sub + c, 1.0, 0.0)
        slot_hit_t[c * 128 : (c + 1) * 128, :] = jnp.concatenate([hit_t, hit_t], axis=1).astype(bf16)
        slot_hit[:, c * 128 : (c + 1) * 128] = jnp.transpose(hit_t).astype(bf16)
    count_col[...] = jnp.transpose(jnp.broadcast_to(obs[2:3, :].astype(f32), (128, 128)))
    land_obs[...] = jnp.zeros_like(land_obs)
    knot_obs[...] = jnp.zeros_like(knot_obs)
    fetches[2].wait()
    fetches[3].wait()

    def finish_sweeps(turn, alpha):
        await_bytes(recv_c.at[turn], rsem_c.at[turn])
        if turn == 0:
            unpack(recv_c[turn], all_c)
        else:
            unpack(recv_c[turn], change_c)
            bends = change_c[pl.ds(19, N_TM, stride=24), :]
            all_c[...] = all_c[...] - alpha * change_c[...]
            all_c[pl.ds(18, N_TM, stride=24), :] = all_c[pl.ds(18, N_TM, stride=24), :] + alpha * alpha * bends
        zero = jnp.zeros((1, 128), f32)

        def onward(t, carry):
            c, acc = carry

            def row(n):
                return all_c[pl.ds(t * 24 + n, 1), :]

            def matrix(n):
                return all_t[pl.ds(t * 72 + n, 1), :]

            for a in range(6):
                c_all[pl.ds(t * 8 + a, 1), :] = c[a]
                first_all[pl.ds(t * 8 + a, 1), :] = row(6 + a) + added(
                    [matrix(36 + a * 6 + b) * c[b] for b in range(6)]
                )
            acc = acc + row(18) + added([row(12 + a) * c[a] for a in range(6)])
            c = tuple(
                row(a) + added([matrix(a * 6 + b) * c[b] for b in range(6)]) for a in range(6)
            )
            return c, acc

        _, acc = lax.fori_loop(0, N_TM, onward, ((zero,) * 6, zero))

        def back(i, carry):
            t = N_TM - 1 - i
            s, acc = carry
            for a in range(6):
                a_all[pl.ds(t * 8 + a, 1), :] = s[a]
            acc = acc + added([all_c[pl.ds(t * 24 + a, 1), :] * s[a] for a in range(6)])
            s = tuple(
                first_all[pl.ds(t * 8 + a, 1), :]
                + added([all_t[pl.ds(t * 72 + b * 6 + a, 1), :] * s[b] for b in range(6)])
                for a in range(6)
            )
            return s, acc

        _, acc = lax.fori_loop(0, N_TM, back, ((zero,) * 6, acc))
        entering = [c_all[pl.ds(me_t * 8 + a, 1), :] for a in range(6)]
        arriving = [a_all[pl.ds(me_t * 8 + a, 1), :] for a in range(6)]
        z = [
            knot_z_local[a * 16 : (a + 1) * 16, :]
            + added([block(g_nat, a, b) * entering[b] for b in range(6)])
            + added([block(b_nat, a, b) * arriving[b] for b in range(6)])
            for a in range(6)
        ]
        return jnp.concatenate(z, axis=0), acc

    def local_sweeps(q):
        w_row[...] = q
        zero = (jnp.zeros((1, 128), f32),) * 6

        def forward(k, carry):
            value = [w_row[pl.ds(a * 16 + k, 1), :] + carry[a] for a in range(6)]
            for a in range(6):
                w_row[pl.ds(a * 16 + k, 1), :] = value[a]
            return tuple(-added([live_row(a, b, k) * value[b] for b in range(6)]) for a in range(6))

        lax.fori_loop(0, 16, forward, zero)
        w = knot_parts(w_row[...])
        for a in range(6):
            z_row[a * 16 : (a + 1) * 16, :] = added([dinv[a, b] * w[b] for b in range(6)])

        def backward(i, carry):
            k = 15 - i
            value = tuple(
                z_row[pl.ds(a * 16 + k, 1), :] - added([live_row(b, a, k) * carry[b] for b in range(6)])
                for a in range(6)
            )
            for a in range(6):
                z_row[pl.ds(a * 16 + k, 1), :] = value[a]
            return value

        lax.fori_loop(0, 16, backward, zero)

    in_block = lax.broadcasted_iota(i32, (GROUP, 32 * GROUP), 1) - 32 * lax.broadcasted_iota(
        i32, (GROUP, 32 * GROUP), 0
    )
    in_block = in_block.astype(f32)
    mod4 = lax.broadcasted_iota(i32, (OBS, 128), 1) % 4

    land_damps = land_parts(land_damp)
    rho, alpha = None, None
    for turn in range(ITERS):
        if turn == 0:
            await_bytes(recv_t, rsem_t)
            unpack(recv_t[...], all_t)
        knot_z, acc = finish_sweeps(turn, alpha)
        last = turn + 1 == ITERS
        filler = jnp.zeros((31, 128), f32)
        expanded[:128, :] = jnp.transpose(jnp.concatenate([knot_z, acc, filler], axis=0))
        mine = pl.ds(pl.multiple_of(first_lane, 16), 16)
        send_z[turn, :16, :] = expanded[mine, :]
        height = 16
        if last:
            height = 32
            expanded[128:256, :] = jnp.transpose(jnp.concatenate([knot_r, acc, filler], axis=0))
            send_z[turn, 16:, :] = expanded[pl.ds(pl.multiple_of(first_lane + 128, 16), 16), :]
        from_z = recv_z.at[turn, pl.ds(0, N_LM * height)]
        exchange_axis(
            send_z.at[turn, pl.ds(0, height)], from_z, height, ssem_z.at[turn], rsem_z.at[turn], False
        )
        await_bytes(recv_a.at[turn], rsem_a.at[turn])
        arrived = [recv_a[turn, pl.ds(j, 128, stride=4), :] for j in range(4)]
        top = jnp.concatenate(arrived[:2], axis=1)
        bottom = jnp.concatenate(arrived[2:], axis=1)
        land_in = [
            dot(slot_hit[:OBS, :], x)[:, :192].astype(bf16)
            for x in split(jnp.concatenate([top, bottom], axis=0))
        ]
        for g in range(OBS // GROUP):
            at = slice(g * GROUP, (g + 1) * GROUP)
            both = dot_nt(
                jnp.concatenate([x[at, :] for x in land_in], axis=0), jl[at].reshape(32 * GROUP, 192)
            )
            sums_l = both[:GROUP] + both[GROUP:]
            sums_z[at, :] = sums_l
        await_bytes(from_z, rsem_z.at[turn])

        def gathered(first):
            return jnp.transpose(
                jnp.concatenate(
                    [recv_z[turn, l * height + first : l * height + first + 16, :] for l in range(N_LM)], axis=0
                )
            )

        knot_z = gathered(0)
        acc, knot_z = knot_z[96:97, :], knot_z[:96, :]
        if last:
            knot_r = gathered(16)[:96, :]

        for i in range(4):
            expanded[pl.ds(i, OBS, stride=4), :] = jnp.where(mod4 == i, knot_z, 0.0)
        knot_in = [dot_nt(knot_hit[:OBS, :], x).astype(bf16) for x in split(expanded[...])]
        for g in range(OBS // GROUP):
            at = slice(g * GROUP, (g + 1) * GROUP)
            both = dot_nt(
                jnp.concatenate([x[at, :] for x in knot_in], axis=0), jk[at].reshape(32 * GROUP, 384)
            )
            sums_z[at, :] = sums_z[at, :] + (both[:GROUP] + both[GROUP:])

        rho_next = total(jnp.where(low128, 0.0, arrived[1])) + jnp.sum(acc, axis=1, keepdims=True)
        if turn == 0:
            knot_p = knot_z
            land_p = land_z
        else:
            beta = rho_next / rho
            knot_p = knot_z + beta * knot_dir[...]
            land_p = [land_z[a] + beta * land_dir[a] for a in range(3)]
        rho = rho_next
        knot_dir[...] = knot_p
        for a in range(3):
            land_dir[a] = land_p[a]
        inner = jnp.zeros((1, 128), f32)
        resids = []
        for g in range(OBS // GROUP):
            at = slice(g * GROUP, (g + 1) * GROUP)
            land_jac = jl[at].reshape(32 * GROUP, 192)
            sums = sums_z[at, :]
            if turn > 0:
                sums = sums + beta * sums_p[at, :]
            if turn + 1 < ITERS:
                sums_p[at, :] = sums
            limit = jnp.concatenate([count_col[at, :]] * (GROUP // 4), axis=1)
            sums = jnp.where((in_block >= 0.0) & (in_block < limit), sums, 0.0)
            resid = sums.astype(bf16)
            product = jnp.sum(sums * resid.astype(f32), axis=0, keepdims=True)
            inner = inner + added([product[:, n * 128 : (n + 1) * 128] for n in range(GROUP // 4)])
            resids.append(resid)
            land_obs[at, :192] = dot(resid, land_jac)
        inner = inner + jnp.sum(
            added([land_damps[a] * land_p[a] * land_p[a] for a in range(3)]), axis=0, keepdims=True
        )
        damp = jnp.concatenate([knot_damp[a] for a in range(6)], axis=0)
        inner = inner + (1.0 / N_LM) * jnp.sum(damp * knot_p * knot_p, axis=0, keepdims=True)

        high, low = split(land_obs[...])
        fill(dot(slot_hit_t[...], jnp.concatenate([high, low], axis=0)), inner, send_b.at[turn])
        far, near = slice(0, 8), slice(8, 16)
        exchange_all(send_b.at[turn], recv_b.at[turn], ssem_b.at[turn], rsem_b.at[turn], far)
        for g in range(OBS // GROUP):
            at = slice(g * GROUP, (g + 1) * GROUP)
            knot_obs[at, :] = dot(resids[g], jk[at].reshape(32 * GROUP, 384))
        high, low = split(knot_obs[...])
        spread = dot(knot_hit_t[...], jnp.concatenate([high, low], axis=0))
        for n in range(3):
            expanded[n * 128 : (n + 1) * 128, :] = jnp.transpose(spread[:, n * 128 : (n + 1) * 128])
        grad = expanded[pl.ds(0, OBS, stride=4), :]
        for i in range(1, 4):
            grad = jnp.where(mod4 == i, expanded[pl.ds(i, OBS, stride=4), :], grad)
        if last:
            send_k[...] = grad.astype(bf16)
            exchange_axis(send_k, recv_k, OBS, ssem_k.at[turn], rsem_k.at[turn], False)
        else:
            send_q[turn] = jnp.transpose(
                jnp.concatenate([grad, jnp.zeros((32, 128), f32)], axis=0)
            ).astype(bf16)
            exchange_axis(
                send_q.at[turn], recv_q.at[turn], 16, ssem_k.at[turn], rsem_k.at[turn], False, True
            )
        exchange_all(send_b.at[turn], recv_b.at[turn], ssem_b.at[turn], rsem_b.at[turn], near)

        if last:
            await_bytes(recv_k, rsem_k.at[turn])
            knot_q = added([recv_k[l * OBS : (l + 1) * OBS, :].astype(f32) for l in range(N_LM)])
            knot_q = knot_q + damp * knot_p
        else:
            await_bytes(recv_q.at[turn], rsem_k.at[turn])
            expanded[:128, :] = jnp.zeros((128, 128), f32)
            expanded[mine, :] = added(
                [recv_q[turn, l * 16 : (l + 1) * 16, :].astype(f32) for l in range(N_LM)]
            )
            knot_q = jnp.transpose(expanded[:128, :])[:96, :] + damp * knot_p
            local_sweeps(knot_q)
            answers = z_row[...]
            slope = knot_q * knot_z_local[...] + knot_r * answers
            send_knots(
                turn + 1,
                summary(knot_parts(knot_q))
                + [jnp.sum(x, axis=0, keepdims=True) for x in (slope, knot_q * answers)],
            )

        await_bytes(recv_b.at[turn], rsem_b.at[turn])
        back = [recv_b[turn, pl.ds(j, 128, stride=4), :] for j in range(4)]
        alpha = rho / total(jnp.where(low128, 0.0, back[1]))
        knot_r = knot_r - alpha * knot_q
        if turn + 1 < ITERS:
            knot_z_local[...] = knot_z_local[...] - alpha * z_row[...]
        pairs = [split(jnp.concatenate(back[2 * c : 2 * c + 2], axis=1)) for c in (0, 1)]
        sums = dot(
            pick_t[...],
            jnp.concatenate([pairs[0][0], pairs[1][0], pairs[0][1], pairs[1][1]], axis=0),
        )
        even, odd = sums[:32], sums[32:]
        land_grad = [
            jnp.where(low32, even[:, :128], swap(odd[:, :128])),
            jnp.where(low32, swap(even[:, :128]), odd[:, :128]),
            jnp.where(low32, even[:, 128:], swap(odd[:, 128:])),
        ]
        land_q = [land_grad[a] + land_damps[a] * land_p[a] for a in range(3)]
        land_r = [land_r[a] - alpha * land_q[a] for a in range(3)]
        if turn + 1 < ITERS:
            land_z = land_apply(land_r)
            to_all(land_z, land_inner(land_r, land_z), send_a.at[turn + 1])
            exchange_all(
                send_a.at[turn + 1], recv_a.at[turn + 1], ssem_a.at[turn + 1], rsem_a.at[turn + 1]
            )
        for a in range(6):
            step = alpha * knot_p[a * 16 : (a + 1) * 16, :]
            knot_step[a] = step if turn == 0 else knot_step[a] + step
        for a in range(3):
            at = slice(a * 32, (a + 1) * 32)
            step = alpha * land_p[a]
            land_step[at, :] = step if turn == 0 else land_step[at, :] + step
    for a in range(6):
        knot_resid[a] = knot_r[a * 16 : (a + 1) * 16, :]
    for a in range(3):
        land_rhs[a * 32 : (a + 1) * 32, :] = land_r[a]
    for j in range(32):
        at = slice(j * 128, (j + 1) * 128)
        land_step_out[:, at] = land_step[pl.ds(j, 3, stride=32), :]
        land_resid_out[:, at] = land_rhs[pl.ds(j, 3, stride=32), :]

    for turn in range(ITERS):
        await_bytes(recv_a.at[turn, pl.ds(0, 4 * (DEVS - 1))], ssem_a.at[turn])
        await_bytes(recv_b.at[turn, pl.ds(0, 4 * (DEVS - 1))], ssem_b.at[turn])
        await_bytes(recv_c.at[turn, pl.ds(0, 3 * (N_TM - 1))], ssem_c.at[turn])
        height = 32 if turn + 1 == ITERS else 16
        await_bytes(recv_z.at[turn, pl.ds(0, height * (N_LM - 1))], ssem_z.at[turn])
        if turn + 1 < ITERS:
            await_bytes(recv_q.at[turn, pl.ds(0, 16 * (N_LM - 1))], ssem_k.at[turn])
    await_bytes(recv_k.at[pl.ds(0, OBS * (N_LM - 1))], ssem_k.at[ITERS - 1])
    await_bytes(recv_t.at[pl.ds(0, 9 * (N_TM - 1))], ssem_t)


def hand_over(*refs):
    for n in range(4):
        refs[4 + n][...] = refs[n][...]


def on_device(
    knot_right_side, land_rhs, jac_knot, jac_land, obs_knot, obs_slot, obs_count, send_list,
    couple, knot_dinv, cuts, land_pinv, knot_damp, land_damp,
):
    vmem = pl.BlockSpec(memory_space=pltpu.VMEM)
    outside = pl.BlockSpec(memory_space=pltpu.HBM)
    knot = jax.ShapeDtypeStruct((6, 16, 128), f32)
    land = jax.ShapeDtypeStruct((3, 4096), f32)
    V = pltpu.VMEM
    dma = pltpu.SemaphoreType.DMA
    outs = pl.pallas_call(
        kernel,
        out_shape=(knot, land, knot, land),
        in_specs=[outside] * 14,
        out_specs=(vmem,) * 4,
        scratch_shapes=[
            V((6, 16, 128), f32),
            V((3, 4096), f32),
            V((OBS, 32, 384), bf16),
            V((OBS, 32, 192), bf16),
            V((1, OBS), i32),
            V((1, OBS), i32),
            V((1, OBS), i32),
            V((2, DEVS), i32),
            V((6, 6, 16, 128), f32),
            V((6, 6, 16, 128), f32),
            V((16, 128), i32),
            V((3, 3, 4096), f32),
            V((6, 16, 128), f32),
            V((3, 4096), f32),
            V((96, 128), f32),
            V((3, 96, 128), f32),
            V((96, 128), f32),
            V((96, 128), f32),
            V((OBS, 32 * GROUP), f32),
            V((OBS, 32 * GROUP), f32),
            V((8, 128), i32),
            V((576, 128), f32),
            V((6, 128, 128), f32),
            V((6, 128, 128), f32),
            V((6, 128, 128), f32),
            V((6, 128, 128), f32),
            V((576, 128), f32),
            V((576, 128), f32),
            V((576, 128), f32),
            V((96, 128), f32),
            V((96, 128), f32),
            V((96, 128), f32),
            V((96, 128), f32),
            V((3, 32, 128), f32),
            V((128, 128), f32),
            V((128, 128), f32),
            V((128, 128), f32),
            V((384, 128), f32),
            V((128, 256), f32),
            V((128, 384), f32),
            V((128, 128), f32),
            V((128, 128), bf16),
            V((128, 256), bf16),
            V((128, 256), bf16),
            V((256, 256), bf16),
            V((256, 128), bf16),
            V((64, 512), bf16),
            V((3, 512, 128), f32),
            V((3, 512, 128), f32),
            V((3, 512, 128), f32),
            V((3, 512, 128), f32),
            V((96, 128), bf16),
            V((768, 128), bf16),
            V((2, 128, 128), bf16),
            V((2, 128, 128), bf16),
            V((3, 3, 128), f32),
            V((3, 48, 128), f32),
            V((9, 128), f32),
            V((144, 128), f32),
            V((3, 32, 128), f32),
            V((3, 256, 128), f32),
            V((24, 128), f32),
            V((72, 128), f32),
            V((384, 128), f32),
            V((384, 128), f32),
            V((1152, 128), f32),
            dma((3,)), dma((3,)), dma((3,)), dma((3,)), dma((3,)), dma((3,)), dma((3,)), dma((3,)),
            dma, dma, dma((3,)), dma((3,)), dma((14,)),
        ],
        compiler_params=pltpu.CompilerParams(
            collective_id=0, has_side_effects=True, vmem_limit_bytes=60 * 1024 * 1024
        ),
    )(
        knot_right_side,
        land_rhs,
        jac_knot,
        jac_land,
        obs_knot.reshape(1, OBS),
        obs_slot.reshape(1, OBS),
        obs_count.reshape(1, OBS),
        send_list.reshape(DEVS, 2).T,
        couple,
        knot_dinv,
        cuts,
        land_pinv,
        knot_damp,
        land_damp,
    )
    return pl.pallas_call(
        hand_over,
        out_shape=(knot, land, knot, land),
        in_specs=[vmem] * 4,
        out_specs=(vmem,) * 4,
        compiler_params=pltpu.CompilerParams(vmem_limit_bytes=60 * 1024 * 1024),
    )(*outs)


def solution(mesh):
    every = ("tm", "lm")
    return jax.shard_map(
        on_device,
        mesh=mesh,
        in_specs=(
            P(None, "tm", None),
            P(None, every),
            P(every, None, None),
            P(every, None, None),
            P(every),
            P(every),
            P(every),
            P(every, None, None),
            P(None, None, "tm", None),
            P(None, None, "tm", None),
            P("tm", None),
            P(None, None, every),
            P(None, "tm", None),
            P(None, every),
        ),
        out_specs=(P(None, "tm", None), P(None, every), P(None, "tm", None), P(None, every)),
        check_vma=False,
    )
```

```python
import jax
import jax.numpy as jnp
from jax import lax
from jax.experimental import pallas as pl
from jax.experimental.pallas import tpu as pltpu
from jax.sharding import PartitionSpec as P

f32, bf16, i32 = jnp.float32, jnp.bfloat16, jnp.int32
MESH = pl.DeviceIdType.MESH
NT_DIMS = (((1,), (1,)), ((), ()))
N_TM, N_LM = 16, 8
DEVS = N_TM * N_LM
ITERS = 3
GROUP = 32
OBS = 96


def dot(a, b):
    return jnp.dot(a, b, preferred_element_type=f32)


def dot_nt(a, b):
    return lax.dot_general(a, b, NT_DIMS, preferred_element_type=f32)


def split(x):
    high = x.astype(bf16)
    return high, (x - high.astype(f32)).astype(bf16)


def swap(x):
    return pltpu.roll(x, 64, 1)


def total(x):
    return jnp.sum(jnp.sum(x, axis=0, keepdims=True), axis=1, keepdims=True)


def kernel(
    *refs,
):
    given, (knot_step, land_step_out, knot_resid, land_resid_out), held = refs[:14], refs[14:18], refs[18:32]
    scratch(given, knot_step, land_step_out, knot_resid, land_resid_out, held, *refs[32:])


def scratch(
    given, knot_step, land_step_out, knot_resid, land_resid_out, held,
    land_rhs, pinv, land_damp, land_step, sums_z, sums_p, fold, obs, live, w_pile, z_pile, u_pile, b_pile, g_nat, u_nat, b_nat, w_row, z_row, knot_z_local, knot_dir,
    land_dir, c_all, a_all, first_all, expanded, land_obs, knot_obs, count_col, knot_hit, knot_hit_t, slot_hit, slot_hit_t,
    pick, pick_t, send_a, recv_a, send_b, recv_b, send_k, recv_k, send_q, recv_q, send_c, recv_c, send_t, recv_t,
    send_z, recv_z, rows_c, rows_t, all_c, change_c, all_t,
    ssem_a, rsem_a, ssem_b, rsem_b, ssem_k, rsem_k, ssem_c, rsem_c, ssem_t, rsem_t, ssem_z, rsem_z, lsem,
):
    me_t, me_l = lax.axis_index("tm"), lax.axis_index("lm")
    me = me_t * N_LM + me_l
    fetches = [pltpu.make_async_copy(x, y, lsem.at[n]) for n, (x, y) in enumerate(zip(given, held))]
    (
        knot_rhs, land_rhs_in, jk, jl, obs_knot, obs_slot, obs_count, send_list,
        couple, dinv, cuts, pinv_in, knot_damp, land_damp_in,
    ) = held

    my_z, my_y = lax.div(me_t, 4), lax.rem(me_t, 4)
    shifts = sorted(
        [(z, y) for z in range(4) for y in range(4)], key=lambda p: -(min(p[0], 4 - p[0]) + min(p[1], 4 - p[1]))
    )

    def wrapped(x, size):
        return jnp.where(x >= size, x - size, x)

    barrier = pltpu.get_barrier_semaphore()
    for shift_z, shift_y in shifts:
        greeted = wrapped(my_z + shift_z, 4) * 4 + wrapped(my_y + shift_y, 4)

        def greet(k, carry, t=greeted):
            pl.semaphore_signal(
                barrier, inc=1, device_id=(t, wrapped(me_l + k, N_LM)), device_id_type=MESH
            )
            return carry

        lax.fori_loop(1 if shift_z == 0 and shift_y == 0 else 0, N_LM, greet, 0)

    for n in (7, 1, 11, 8, 10, 0, 9, 4, 5, 6, 12, 13, 2, 3):
        fetches[n].start()

    def exchange_all(send, recv, ssem, rsem, part=slice(None)):
        at = recv.at[pl.ds(me * 4, 4)]
        for shift_z, shift_y in shifts[part]:
            t = wrapped(my_z + shift_z, 4) * 4 + wrapped(my_y + shift_y, 4)

            def to(k, carry, t=t):
                l = wrapped(me_l + k, N_LM)
                pltpu.make_async_remote_copy(
                    send.at[pl.ds((t * N_LM + l) * 4, 4)], at, ssem, rsem,
                    device_id=(t, l), device_id_type=MESH,
                ).start()
                return carry

            here = shift_z == 0 and shift_y == 0
            lax.fori_loop(1 if here else 0, N_LM, to, 0)
            if here:
                pltpu.make_async_copy(send.at[pl.ds(me * 4, 4)], at, rsem).start()

    def exchange_axis(send, recv, rows, ssem, rsem, over_tm, scattered=False):
        size, mine = (N_TM, me_t) if over_tm else (N_LM, me_l)
        at = recv.at[pl.ds(pl.multiple_of(mine * rows, rows), rows)]

        def part(d):
            return send.at[pl.ds(pl.multiple_of(d * rows, rows), rows)] if scattered else send

        def to(k, carry):
            d = wrapped(mine + k, size)
            pltpu.make_async_remote_copy(
                part(d), at, ssem, rsem,
                device_id=(d, me_l) if over_tm else (me_t, d), device_id_type=MESH,
            ).start()
            return carry

        lax.fori_loop(1, size, to, 0)
        pltpu.make_async_copy(part(mine), at, rsem).start()

    def await_bytes(like, sem):
        pltpu.make_async_copy(like, like, sem).wait()

    lane = lax.broadcasted_iota(i32, (128, 128), 1)
    sub = lax.broadcasted_iota(i32, (128, 128), 0)
    low32 = lax.broadcasted_iota(i32, (32, 128), 1) < 64
    low128 = lane < 64

    first_lane = me_l * 16

    def packed(ref, rows):
        group = lax.broadcasted_iota(i32, (rows // 8, 128), 1) // 16
        out = jnp.zeros((rows // 8, 128), f32)
        for j in range(8):
            turned = pltpu.roll(ref[pl.ds(j, rows // 8, stride=8), :], wrapped(16 * j + 128 - first_lane, 128), 1)
            out = jnp.where(group == j, turned, out)
        return out

    def unpack(packs, ref):
        rows = packs.shape[0]
        mine = lax.broadcasted_iota(i32, (rows, 128), 1) // 16 == me_l
        for j in range(8):
            turned = pltpu.roll(packs, wrapped(first_lane + 128 - 16 * j, 128), 1)
            ref[pl.ds(j, rows, stride=8), :] = jnp.where(mine, turned, 0.0)

    def land_apply(r):
        return [
            pinv[a, 0:32, :] * r[0] + pinv[a, 32:64, :] * r[1] + pinv[a, 64:96, :] * r[2] for a in range(3)
        ]

    def land_inner(x, y):
        s = x[0] * y[0] + x[1] * y[1] + x[2] * y[2]
        return jnp.sum(s, axis=0, keepdims=True)

    def to_all(z, partial, send):
        even = (jnp.where(low32, z[0], swap(z[1])), jnp.where(low32, z[2], 0.0))
        odd = (jnp.where(low32, swap(z[0]), z[1]), jnp.where(low32, swap(z[2]), 0.0))
        tiles = jnp.concatenate(
            [jnp.concatenate(even, axis=1), jnp.concatenate(odd, axis=1)], axis=0
        )
        high, low = split(tiles)
        out = dot(pick[...], jnp.concatenate([high, low], axis=0))
        fill(out, partial, send)

    def fill(out, partial, send):
        extra = jnp.broadcast_to(partial + swap(partial), (128, 128))
        send[pl.ds(0, 128, stride=4), :] = out[:128, :128]
        send[pl.ds(1, 128, stride=4), :] = jnp.where(low128, out[:128, 128:], extra)
        send[pl.ds(2, 128, stride=4), :] = out[128:, :128]
        send[pl.ds(3, 128, stride=4), :] = out[128:, 128:]

    fetches[7].wait()
    for c in (0, 1):
        code = 2 * (sub % 32) + (sub // 32) % 2
        hit_t = jnp.where(send_list[c : c + 1, :] == code, 1.0, 0.0)
        pick[c * 128 : (c + 1) * 128, :] = jnp.transpose(hit_t).astype(bf16)
        hit_t = hit_t[:64, :].astype(bf16)
        pick_t[:, c * 128 : (c + 1) * 128] = hit_t
        pick_t[:, 256 + c * 128 : 256 + (c + 1) * 128] = hit_t
    fetches[1].wait()
    fetches[11].wait()
    for j in range(32):
        at = slice(j * 128, (j + 1) * 128)
        land_rhs[pl.ds(j, 3, stride=32), :] = land_rhs_in[:, at]
        for a in range(3):
            pinv[a, pl.ds(j, 3, stride=32), :] = pinv_in[a, :, at]

    def land_parts(ref):
        return [ref[a * 32 : (a + 1) * 32, :] for a in range(3)]

    land_r = land_parts(land_rhs)
    land_z = land_apply(land_r)
    to_all(land_z, land_inner(land_r, land_z), send_a.at[0])

    for n in (8, 10, 0, 9):
        fetches[n].wait()
    open_ends = 1.0 - cuts[...].astype(f32)
    for a in range(6):
        for b in range(6):
            live[(a * 6 + b) * 16 : (a * 6 + b + 1) * 16, :] = couple[a, b] * open_ends
    column = lax.broadcasted_iota(i32, (8, 128), 0)
    unit = tuple(jnp.where(column == a, 1.0, 0.0) for a in range(6))
    none = tuple(jnp.zeros((8, 128), f32) for _ in range(6))

    def live_row(a, b, k):
        return live[pl.ds((a * 6 + b) * 16 + k, 1), :]

    def added(terms):
        terms = list(terms)
        while len(terms) > 1:
            terms = [x + y for x, y in zip(terms[::2], terms[1::2])] + (
                [terms[-1]] if len(terms) % 2 else []
            )
        return terms[0]

    def forward_columns(k, carry):
        at = pl.ds(pl.multiple_of(k * 8, 8), 8)
        value = [carry[a] + jnp.where(column == 6, knot_rhs[a, pl.ds(k, 1), :], 0.0) for a in range(6)]
        for a in range(6):
            w_pile[a, at, :] = value[a]
        return tuple(-added(live_row(a, b, k) * value[b] for b in range(6)) for a in range(6))

    through = lax.fori_loop(0, 16, forward_columns, unit)

    def backward_columns(i, carry):
        k = 15 - i
        at = pl.ds(pl.multiple_of(k * 8, 8), 8)
        z, u, s = carry
        w = [w_pile[b, at, :] for b in range(6)]
        rows = [[live_row(b, a, k) for b in range(6)] for a in range(6)]
        z = tuple(
            added([dinv[a, b, pl.ds(k, 1), :] * w[b] for b in range(6)])
            - added([rows[a][b] * z[b] for b in range(6)])
            for a in range(6)
        )
        u = tuple(
            added([dinv[b, a, pl.ds(k, 1), :] * w[b] for b in range(6)])
            - added([rows[a][b] * u[b] for b in range(6)])
            for a in range(6)
        )
        s = tuple(-added([rows[a][b] * s[b] for b in range(6)]) for a in range(6))
        for a in range(6):
            z_pile[a, at, :] = z[a]
            u_pile[a, at, :] = u[a]
            b_pile[a, at, :] = s[a]
        return z, u, s

    entry, _, _ = lax.fori_loop(0, 16, backward_columns, (none, none, unit))
    for a in range(6):
        rows_t[a * 6 : a * 6 + 6, :] = through[a][:6]
        rows_t[36 + a * 6 : 36 + a * 6 + 6, :] = entry[a][:6]
        for b in range(6):
            at = slice((a * 6 + b) * 16, (a * 6 + b + 1) * 16)
            g_nat[at, :] = z_pile[a, pl.ds(b, 16, stride=8), :]
            u_nat[at, :] = u_pile[a, pl.ds(b, 16, stride=8), :]
            b_nat[at, :] = b_pile[a, pl.ds(b, 16, stride=8), :]
        knot_z_local[a * 16 : (a + 1) * 16, :] = z_pile[a, pl.ds(6, 16, stride=8), :]

    def block(ref, a, b):
        return ref[(a * 6 + b) * 16 : (a * 6 + b + 1) * 16, :]

    def summary(r):
        return [
            jnp.sum(added([block(ref, b, a) * r[b] for b in range(6)]), axis=0, keepdims=True)
            for ref in (b_nat, u_nat, g_nat)
            for a in range(6)
        ]

    def knot_parts(x):
        return [x[a * 16 : (a + 1) * 16, :] for a in range(6)]

    knot_r = jnp.concatenate([knot_rhs[a] for a in range(6)], axis=0)
    passed_on = summary(knot_parts(knot_r))

    def send_knots(turn, rows):
        for n, row in enumerate(rows):
            rows_c[n : n + 1, :] = row
        send_c[turn] = packed(rows_c, 24)
        exchange_axis(send_c.at[turn], recv_c.at[turn], 3, ssem_c.at[turn], rsem_c.at[turn], True)

    rows_c[...] = jnp.zeros_like(rows_c)
    send_t[...] = packed(rows_t, 72)
    own = jnp.sum(knot_r * knot_z_local[...], axis=0, keepdims=True)

    pl.semaphore_wait(barrier, DEVS - 1)
    exchange_axis(send_t, recv_t, 9, ssem_t, rsem_t, True)
    send_knots(0, passed_on + [own])
    exchange_all(send_a.at[0], recv_a.at[0], ssem_a.at[0], rsem_a.at[0])

    for n in (4, 5, 6, 12, 13):
        fetches[n].wait()
    for j in range(32):
        land_damp[pl.ds(j, 3, stride=32), :] = land_damp_in[:, j * 128 : (j + 1) * 128]
    obs[...] = jnp.full((8, 128), -1, i32)
    obs[0:1, 0:OBS] = obs_knot[...]
    obs[1:2, 0:OBS] = obs_slot[...]
    obs[2:3, 0:OBS] = obs_count[...]
    hit_t = jnp.where(obs[0:1, :] == sub // 4, 1.0, 0.0)
    knot_hit_t[...] = jnp.concatenate([hit_t, hit_t], axis=1).astype(bf16)
    knot_hit[...] = jnp.transpose(hit_t).astype(bf16)
    for c in (0, 1):
        hit_t = jnp.where(obs[1:2, :] == 2 * sub + c, 1.0, 0.0)
        slot_hit_t[c * 128 : (c + 1) * 128, :] = jnp.concatenate([hit_t, hit_t], axis=1).astype(bf16)
        slot_hit[:, c * 128 : (c + 1) * 128] = jnp.transpose(hit_t).astype(bf16)
    count_col[...] = jnp.transpose(jnp.broadcast_to(obs[2:3, :].astype(f32), (128, 128)))
    land_obs[...] = jnp.zeros_like(land_obs)
    knot_obs[...] = jnp.zeros_like(knot_obs)
    fetches[2].wait()
    fetches[3].wait()

    def finish_sweeps(turn, alpha):
        await_bytes(recv_c.at[turn], rsem_c.at[turn])
        if turn == 0:
            unpack(recv_c[turn], all_c)
        else:
            unpack(recv_c[turn], change_c)
            bends = change_c[pl.ds(19, N_TM, stride=24), :]
            all_c[...] = all_c[...] - alpha * change_c[...]
            all_c[pl.ds(18, N_TM, stride=24), :] = all_c[pl.ds(18, N_TM, stride=24), :] + alpha * alpha * bends
        zero = jnp.zeros((1, 128), f32)

        def onward(t, carry):
            c, acc = carry

            def row(n):
                return all_c[pl.ds(t * 24 + n, 1), :]

            def matrix(n):
                return all_t[pl.ds(t * 72 + n, 1), :]

            for a in range(6):
                c_all[pl.ds(t * 8 + a, 1), :] = c[a]
                first_all[pl.ds(t * 8 + a, 1), :] = row(6 + a) + added(
                    [matrix(36 + a * 6 + b) * c[b] for b in range(6)]
                )
            acc = acc + row(18) + added([row(12 + a) * c[a] for a in range(6)])
            c = tuple(
                row(a) + added([matrix(a * 6 + b) * c[b] for b in range(6)]) for a in range(6)
            )
            return c, acc

        _, acc = lax.fori_loop(0, N_TM, onward, ((zero,) * 6, zero), unroll=4)

        def back(i, carry):
            t = N_TM - 1 - i
            s, acc = carry
            for a in range(6):
                a_all[pl.ds(t * 8 + a, 1), :] = s[a]
            acc = acc + added([all_c[pl.ds(t * 24 + a, 1), :] * s[a] for a in range(6)])
            s = tuple(
                first_all[pl.ds(t * 8 + a, 1), :]
                + added([all_t[pl.ds(t * 72 + b * 6 + a, 1), :] * s[b] for b in range(6)])
                for a in range(6)
            )
            return s, acc

        _, acc = lax.fori_loop(0, N_TM, back, ((zero,) * 6, acc), unroll=4)
        entering = [c_all[pl.ds(me_t * 8 + a, 1), :] for a in range(6)]
        arriving = [a_all[pl.ds(me_t * 8 + a, 1), :] for a in range(6)]
        z = [
            knot_z_local[a * 16 : (a + 1) * 16, :]
            + added([block(g_nat, a, b) * entering[b] for b in range(6)])
            + added([block(b_nat, a, b) * arriving[b] for b in range(6)])
            for a in range(6)
        ]
        return jnp.concatenate(z, axis=0), acc

    def local_sweeps(q):
        w_row[...] = q
        zero = (jnp.zeros((1, 128), f32),) * 6

        def forward(k, carry):
            value = [w_row[pl.ds(a * 16 + k, 1), :] + carry[a] for a in range(6)]
            for a in range(6):
                w_row[pl.ds(a * 16 + k, 1), :] = value[a]
            return tuple(-added([live_row(a, b, k) * value[b] for b in range(6)]) for a in range(6))

        lax.fori_loop(0, 16, forward, zero, unroll=4)
        w = knot_parts(w_row[...])
        for a in range(6):
            z_row[a * 16 : (a + 1) * 16, :] = added([dinv[a, b] * w[b] for b in range(6)])

        def backward(i, carry):
            k = 15 - i
            value = tuple(
                z_row[pl.ds(a * 16 + k, 1), :] - added([live_row(b, a, k) * carry[b] for b in range(6)])
                for a in range(6)
            )
            for a in range(6):
                z_row[pl.ds(a * 16 + k, 1), :] = value[a]
            return value

        lax.fori_loop(0, 16, backward, zero, unroll=4)

    in_block = lax.broadcasted_iota(i32, (GROUP, 32 * GROUP), 1) - 32 * lax.broadcasted_iota(
        i32, (GROUP, 32 * GROUP), 0
    )
    in_block = in_block.astype(f32)
    mod4 = lax.broadcasted_iota(i32, (OBS, 128), 1) % 4
    of_vehicle = (
        lax.broadcasted_iota(i32, (128, 384), 1) % 4 == lax.broadcasted_iota(i32, (128, 384), 0) % 4
    )
    fold[...] = jnp.where(
        lax.broadcasted_iota(i32, (384, 128), 0) // 4 == lax.broadcasted_iota(i32, (384, 128), 1), 1.0, 0.0
    ).astype(bf16)

    land_damps = land_parts(land_damp)
    rho, alpha = None, None
    for turn in range(ITERS):
        if turn == 0:
            await_bytes(recv_t, rsem_t)
            unpack(recv_t[...], all_t)
        knot_z, acc = finish_sweeps(turn, alpha)
        last = turn + 1 == ITERS
        filler = jnp.zeros((31, 128), f32)
        expanded[:128, :] = jnp.transpose(jnp.concatenate([knot_z, acc, filler], axis=0))
        mine = pl.ds(pl.multiple_of(first_lane, 16), 16)
        send_z[turn, :16, :] = expanded[mine, :]
        height = 16
        if last:
            height = 32
            expanded[128:256, :] = jnp.transpose(jnp.concatenate([knot_r, acc, filler], axis=0))
            send_z[turn, 16:, :] = expanded[pl.ds(pl.multiple_of(first_lane + 128, 16), 16), :]
        from_z = recv_z.at[turn, pl.ds(0, N_LM * height)]
        exchange_axis(
            send_z.at[turn, pl.ds(0, height)], from_z, height, ssem_z.at[turn], rsem_z.at[turn], False
        )
        await_bytes(recv_a.at[turn], rsem_a.at[turn])
        arrived = [recv_a[turn, pl.ds(j, 128, stride=4), :] for j in range(4)]
        top = jnp.concatenate(arrived[:2], axis=1)
        bottom = jnp.concatenate(arrived[2:], axis=1)
        land_in = [
            dot(slot_hit[:OBS, :], x)[:, :192].astype(bf16)
            for x in split(jnp.concatenate([top, bottom], axis=0))
        ]
        for g in range(OBS // GROUP):
            at = slice(g * GROUP, (g + 1) * GROUP)
            both = dot_nt(
                jnp.concatenate([x[at, :] for x in land_in], axis=0), jl[at].reshape(32 * GROUP, 192)
            )
            sums_l = both[:GROUP] + both[GROUP:]
            sums_z[at, :] = sums_l
        await_bytes(from_z, rsem_z.at[turn])

        def gathered(first):
            return jnp.transpose(
                jnp.concatenate(
                    [recv_z[turn, l * height + first : l * height + first + 16, :] for l in range(N_LM)], axis=0
                )
            )

        knot_z = gathered(0)
        acc, knot_z = knot_z[96:97, :], knot_z[:96, :]
        if last:
            knot_r = gathered(16)[:96, :]

        for i in range(4):
            expanded[pl.ds(i, OBS, stride=4), :] = jnp.where(mod4 == i, knot_z, 0.0)
        knot_in = [dot_nt(knot_hit[:OBS, :], x).astype(bf16) for x in split(expanded[...])]
        for g in range(OBS // GROUP):
            at = slice(g * GROUP, (g + 1) * GROUP)
            both = dot_nt(
                jnp.concatenate([x[at, :] for x in knot_in], axis=0), jk[at].reshape(32 * GROUP, 384)
            )
            sums_z[at, :] = sums_z[at, :] + (both[:GROUP] + both[GROUP:])

        rho_next = total(jnp.where(low128, 0.0, arrived[1])) + jnp.sum(acc, axis=1, keepdims=True)
        if turn == 0:
            knot_p = knot_z
            land_p = land_z
        else:
            beta = rho_next / rho
            knot_p = knot_z + beta * knot_dir[...]
            land_p = [land_z[a] + beta * land_dir[a] for a in range(3)]
        rho = rho_next
        knot_dir[...] = knot_p
        for a in range(3):
            land_dir[a] = land_p[a]
        inner = jnp.zeros((1, 128), f32)
        resids = []
        for g in range(OBS // GROUP):
            at = slice(g * GROUP, (g + 1) * GROUP)
            land_jac = jl[at].reshape(32 * GROUP, 192)
            sums = sums_z[at, :]
            if turn > 0:
                sums = sums + beta * sums_p[at, :]
            if turn + 1 < ITERS:
                sums_p[at, :] = sums
            limit = jnp.concatenate([count_col[at, :]] * (GROUP // 4), axis=1)
            sums = jnp.where((in_block >= 0.0) & (in_block < limit), sums, 0.0)
            resid = sums.astype(bf16)
            product = jnp.sum(sums * resid.astype(f32), axis=0, keepdims=True)
            inner = inner + added([product[:, n * 128 : (n + 1) * 128] for n in range(GROUP // 4)])
            resids.append(resid)
            land_obs[at, :192] = dot(resid, land_jac)
        inner = inner + jnp.sum(
            added([land_damps[a] * land_p[a] * land_p[a] for a in range(3)]), axis=0, keepdims=True
        )
        damp = jnp.concatenate([knot_damp[a] for a in range(6)], axis=0)
        inner = inner + (1.0 / N_LM) * jnp.sum(damp * knot_p * knot_p, axis=0, keepdims=True)

        high, low = split(land_obs[...])
        fill(dot(slot_hit_t[...], jnp.concatenate([high, low], axis=0)), inner, send_b.at[turn])
        far, near = slice(0, 8), slice(8, 16)
        exchange_all(send_b.at[turn], recv_b.at[turn], ssem_b.at[turn], rsem_b.at[turn], far)
        for g in range(OBS // GROUP):
            at = slice(g * GROUP, (g + 1) * GROUP)
            knot_obs[at, :] = dot(resids[g], jk[at].reshape(32 * GROUP, 384))
        high, low = split(knot_obs[...])
        spread = dot(knot_hit_t[...], jnp.concatenate([high, low], axis=0))
        if last:
            for n in range(3):
                expanded[n * 128 : (n + 1) * 128, :] = jnp.transpose(spread[:, n * 128 : (n + 1) * 128])
            grad = expanded[pl.ds(0, OBS, stride=4), :]
            for i in range(1, 4):
                grad = jnp.where(mod4 == i, expanded[pl.ds(i, OBS, stride=4), :], grad)
            send_k[...] = grad.astype(bf16)
            exchange_axis(send_k, recv_k, OBS, ssem_k.at[turn], rsem_k.at[turn], False)
        else:
            spread = jnp.where(of_vehicle, spread, 0.0).astype(bf16)
            send_q[turn] = dot(spread, fold[...]).astype(bf16)
            exchange_axis(
                send_q.at[turn], recv_q.at[turn], 16, ssem_k.at[turn], rsem_k.at[turn], False, True
            )
        exchange_all(send_b.at[turn], recv_b.at[turn], ssem_b.at[turn], rsem_b.at[turn], near)

        if last:
            await_bytes(recv_k, rsem_k.at[turn])
            knot_q = added([recv_k[l * OBS : (l + 1) * OBS, :].astype(f32) for l in range(N_LM)])
            knot_q = knot_q + damp * knot_p
        else:
            await_bytes(recv_q.at[turn], rsem_k.at[turn])
            expanded[:128, :] = jnp.zeros((128, 128), f32)
            expanded[mine, :] = added(
                [recv_q[turn, l * 16 : (l + 1) * 16, :].astype(f32) for l in range(N_LM)]
            )
            knot_q = jnp.transpose(expanded[:128, :])[:96, :] + damp * knot_p
            local_sweeps(knot_q)
            answers = z_row[...]
            slope = knot_q * knot_z_local[...] + knot_r * answers
            send_knots(
                turn + 1,
                summary(knot_parts(knot_q))
                + [jnp.sum(x, axis=0, keepdims=True) for x in (slope, knot_q * answers)],
            )

        await_bytes(recv_b.at[turn], rsem_b.at[turn])
        back = [recv_b[turn, pl.ds(j, 128, stride=4), :] for j in range(4)]
        alpha = rho / total(jnp.where(low128, 0.0, back[1]))
        knot_r = knot_r - alpha * knot_q
        if turn + 1 < ITERS:
            knot_z_local[...] = knot_z_local[...] - alpha * z_row[...]
        pairs = [split(jnp.concatenate(back[2 * c : 2 * c + 2], axis=1)) for c in (0, 1)]
        sums = dot(
            pick_t[...],
            jnp.concatenate([pairs[0][0], pairs[1][0], pairs[0][1], pairs[1][1]], axis=0),
        )
        even, odd = sums[:32], sums[32:]
        land_grad = [
            jnp.where(low32, even[:, :128], swap(odd[:, :128])),
            jnp.where(low32, swap(even[:, :128]), odd[:, :128]),
            jnp.where(low32, even[:, 128:], swap(odd[:, 128:])),
        ]
        land_q = [land_grad[a] + land_damps[a] * land_p[a] for a in range(3)]
        land_r = [land_r[a] - alpha * land_q[a] for a in range(3)]
        if turn + 1 < ITERS:
            land_z = land_apply(land_r)
            to_all(land_z, land_inner(land_r, land_z), send_a.at[turn + 1])
            exchange_all(
                send_a.at[turn + 1], recv_a.at[turn + 1], ssem_a.at[turn + 1], rsem_a.at[turn + 1]
            )
        for a in range(6):
            step = alpha * knot_p[a * 16 : (a + 1) * 16, :]
            knot_step[a] = step if turn == 0 else knot_step[a] + step
        for a in range(3):
            at = slice(a * 32, (a + 1) * 32)
            step = alpha * land_p[a]
            land_step[at, :] = step if turn == 0 else land_step[at, :] + step
    for a in range(6):
        knot_resid[a] = knot_r[a * 16 : (a + 1) * 16, :]
    for a in range(3):
        land_rhs[a * 32 : (a + 1) * 32, :] = land_r[a]
    for j in range(32):
        at = slice(j * 128, (j + 1) * 128)
        land_step_out[:, at] = land_step[pl.ds(j, 3, stride=32), :]
        land_resid_out[:, at] = land_rhs[pl.ds(j, 3, stride=32), :]

    for turn in range(ITERS):
        await_bytes(recv_a.at[turn, pl.ds(0, 4 * (DEVS - 1))], ssem_a.at[turn])
        await_bytes(recv_b.at[turn, pl.ds(0, 4 * (DEVS - 1))], ssem_b.at[turn])
        await_bytes(recv_c.at[turn, pl.ds(0, 3 * (N_TM - 1))], ssem_c.at[turn])
        height = 32 if turn + 1 == ITERS else 16
        await_bytes(recv_z.at[turn, pl.ds(0, height * (N_LM - 1))], ssem_z.at[turn])
        if turn + 1 < ITERS:
            await_bytes(recv_q.at[turn, pl.ds(0, 16 * (N_LM - 1))], ssem_k.at[turn])
    await_bytes(recv_k.at[pl.ds(0, OBS * (N_LM - 1))], ssem_k.at[ITERS - 1])
    await_bytes(recv_t.at[pl.ds(0, 9 * (N_TM - 1))], ssem_t)


def hand_over(*refs):
    for n in range(4):
        refs[4 + n][...] = refs[n][...]


def on_device(
    knot_right_side, land_rhs, jac_knot, jac_land, obs_knot, obs_slot, obs_count, send_list,
    couple, knot_dinv, cuts, land_pinv, knot_damp, land_damp,
):
    vmem = pl.BlockSpec(memory_space=pltpu.VMEM)
    outside = pl.BlockSpec(memory_space=pltpu.HBM)
    knot = jax.ShapeDtypeStruct((6, 16, 128), f32)
    land = jax.ShapeDtypeStruct((3, 4096), f32)
    V = pltpu.VMEM
    dma = pltpu.SemaphoreType.DMA
    outs = pl.pallas_call(
        kernel,
        out_shape=(knot, land, knot, land),
        in_specs=[outside] * 14,
        out_specs=(vmem,) * 4,
        scratch_shapes=[
            V((6, 16, 128), f32),
            V((3, 4096), f32),
            V((OBS, 32, 384), bf16),
            V((OBS, 32, 192), bf16),
            V((1, OBS), i32),
            V((1, OBS), i32),
            V((1, OBS), i32),
            V((2, DEVS), i32),
            V((6, 6, 16, 128), f32),
            V((6, 6, 16, 128), f32),
            V((16, 128), i32),
            V((3, 3, 4096), f32),
            V((6, 16, 128), f32),
            V((3, 4096), f32),
            V((96, 128), f32),
            V((3, 96, 128), f32),
            V((96, 128), f32),
            V((96, 128), f32),
            V((OBS, 32 * GROUP), f32),
            V((OBS, 32 * GROUP), f32),
            V((384, 128), bf16),
            V((8, 128), i32),
            V((576, 128), f32),
            V((6, 128, 128), f32),
            V((6, 128, 128), f32),
            V((6, 128, 128), f32),
            V((6, 128, 128), f32),
            V((576, 128), f32),
            V((576, 128), f32),
            V((576, 128), f32),
            V((96, 128), f32),
            V((96, 128), f32),
            V((96, 128), f32),
            V((96, 128), f32),
            V((3, 32, 128), f32),
            V((128, 128), f32),
            V((128, 128), f32),
            V((128, 128), f32),
            V((384, 128), f32),
            V((128, 256), f32),
            V((128, 384), f32),
            V((128, 128), f32),
            V((128, 128), bf16),
            V((128, 256), bf16),
            V((128, 256), bf16),
            V((256, 256), bf16),
            V((256, 128), bf16),
            V((64, 512), bf16),
            V((3, 512, 128), f32),
            V((3, 512, 128), f32),
            V((3, 512, 128), f32),
            V((3, 512, 128), f32),
            V((96, 128), bf16),
            V((768, 128), bf16),
            V((2, 128, 128), bf16),
            V((2, 128, 128), bf16),
            V((3, 3, 128), f32),
            V((3, 48, 128), f32),
            V((9, 128), f32),
            V((144, 128), f32),
            V((3, 32, 128), f32),
            V((3, 256, 128), f32),
            V((24, 128), f32),
            V((72, 128), f32),
            V((384, 128), f32),
            V((384, 128), f32),
            V((1152, 128), f32),
            dma((3,)), dma((3,)), dma((3,)), dma((3,)), dma((3,)), dma((3,)), dma((3,)), dma((3,)),
            dma, dma, dma((3,)), dma((3,)), dma((14,)),
        ],
        compiler_params=pltpu.CompilerParams(
            collective_id=0, has_side_effects=True, vmem_limit_bytes=60 * 1024 * 1024
        ),
    )(
        knot_right_side,
        land_rhs,
        jac_knot,
        jac_land,
        obs_knot.reshape(1, OBS),
        obs_slot.reshape(1, OBS),
        obs_count.reshape(1, OBS),
        send_list.reshape(DEVS, 2).T,
        couple,
        knot_dinv,
        cuts,
        land_pinv,
        knot_damp,
        land_damp,
    )
    return pl.pallas_call(
        hand_over,
        out_shape=(knot, land, knot, land),
        in_specs=[vmem] * 4,
        out_specs=(vmem,) * 4,
        compiler_params=pltpu.CompilerParams(vmem_limit_bytes=60 * 1024 * 1024),
    )(*outs)


def solution(mesh):
    every = ("tm", "lm")
    return jax.shard_map(
        on_device,
        mesh=mesh,
        in_specs=(
            P(None, "tm", None),
            P(None, every),
            P(every, None, None),
            P(every, None, None),
            P(every),
            P(every),
            P(every),
            P(every, None, None),
            P(None, None, "tm", None),
            P(None, None, "tm", None),
            P("tm", None),
            P(None, None, every),
            P(None, "tm", None),
            P(None, every),
        ),
        out_specs=(P(None, "tm", None), P(None, every), P(None, "tm", None), P(None, every)),
        check_vma=False,
    )
```
